32 devices in a mesh: layer: 4 (over y, x), lat: 8 (over z, core).
Axes of the slice: x: 2, y: 2, z: 4, core: 2. Of those that a mesh axis runs over, the one named last changes fastest.
Arguments:
- positions: float32 [3, 131072], P(None, ('layer', 'lat')), may hold values from 0 to 6
- velocities: float32 [3, 131072], P(None, ('layer', 'lat')), may hold values from -6 to 6
- types: int32 [131072], P(('layer', 'lat')), may hold values from 0 to 1
- counts: int32 [1024], P(('layer', 'lat')), may hold values from 0 to 128, as said below
- a_table: float32 [2, 2], replicated, may hold values from -60 to -20
- local_nbr: int32 [1024, 2], P(('layer', 'lat')), may hold values from -1 to 31, as said below
- face_nbr: int32 [1024, 2], P(('layer', 'lat')), may hold values from -1 to 7, as said below
- cross_send: int32 [32, 5, 12], P(('layer', 'lat')), may hold values from -1 to 15, as said below
- cross_pair: int32 [1024, 2], P(('layer', 'lat')), may hold values from -1 to 59, as said below
Outputs:
- new_positions: float32 [3, 131072], P(None, ('layer', 'lat'))
- new_velocities: float32 [3, 131072], P(None, ('layer', 'lat'))
The draws below stay inside these ranges and needn't reach their ends.
Inputs may be any that keep to these rules, and one draw needn't show every extreme that they name: `counts`: some tile holds 128 beads and some none in every draw. `local_nbr`: each row lists distinct tiles of the same device, each with a higher index than the row's tile and within 8 of it, or -1. `face_nbr`: entries index the first 8 tiles of the device one place lower along lat (cyclically) in the same layer; distinct within a row, or -1. `cross_send`: entry [d, o, c] names a top tile (numbered among the last 16 tiles of device d) that device d offers to the device of the next layer at lateral offset o - 2, cyclically; -1 marks an empty slot; entries are distinct within [d, o]; for o = 2 every slot is used. `cross_pair`: entries are ghost slots o * 12 + c, distinct within a row, or -1.
All inputs are finite; a program needn't handle non-finite values.
Results may differ from the reference program's by a relative error of at most 0.0003.
Values sent between devices are 32-bit elements; how exact they have to be, the bound alone decides.
No kernel may reach another device: no remote copies, remote signals or barrier semaphores. Data moves between devices by JAX's collectives and lax.ppermute only.
A program may use at most 64 MiB of HBM per device.

```python
import functools
import math
import jax
import jax.numpy as jnp
from jax import lax

TILE = 128
TILES_DEV = 32
NTYPE = 2
NL = 2
NF = 2
NC = 2
REACH = 2
CAP = 12
FACE = 8
UP = 16
NOFF = 5
SLOTS = 60
TILES_ALL = 1024
BEADS = 131072
N_LAYER = 4
N_LAT = 8


def draw_counts(key, part):
    first, second, third = jax.random.split(key, 3)
    tile_index = jnp.arange(TILES_ALL, dtype=jnp.int32)
    layer_place = tile_index // (TILES_DEV * N_LAT)
    liquid = (layer_place >= 1) & (layer_place <= N_LAYER - 2)
    dense = jax.random.randint(first, (TILES_ALL,), 48, TILE + 1, dtype=jnp.int32)
    sparse = jax.random.randint(second, (TILES_ALL,), 0, 41, dtype=jnp.int32)
    empty = jax.random.randint(third, (TILES_ALL,), 0, 2, dtype=jnp.int32) == 0
    filled = jnp.where(liquid, dense, jnp.where(empty, 0, sparse))
    return jnp.where(liquid & (tile_index % TILES_DEV == 0), TILE, filled).astype(jnp.int32)


def draw_local_nbr(key, part):
    first, second = jax.random.split(key)
    scores = jax.random.randint(first, (TILES_ALL, 8), 0, 1 << 20, dtype=jnp.int32) * 8 + jnp.arange(8, dtype=jnp.int32)
    order = jnp.argsort(scores, axis=1)[:, :NL].astype(jnp.int32)
    target = (jnp.arange(TILES_ALL, dtype=jnp.int32) % TILES_DEV)[:, None] + order + 1
    keep = (target < TILES_DEV) & (jax.random.randint(second, (TILES_ALL, NL), 0, 4, dtype=jnp.int32) != 0)
    return jnp.where(keep, target, -1).astype(jnp.int32)


def draw_face_nbr(key, part):
    first, second = jax.random.split(key)
    scores = jax.random.randint(first, (TILES_ALL, FACE), 0, 1 << 20, dtype=jnp.int32) * FACE + jnp.arange(FACE, dtype=jnp.int32)
    order = jnp.argsort(scores, axis=1)[:, :NF].astype(jnp.int32)
    keep = jax.random.randint(second, (TILES_ALL, NF), 0, 4, dtype=jnp.int32) != 0
    return jnp.where(keep, order, -1).astype(jnp.int32)


def draw_cross_send(key, part):
    first, second = jax.random.split(key)
    devices_count = TILES_ALL // TILES_DEV
    scores = jax.random.randint(first, (devices_count, NOFF, UP), 0, 1 << 20, dtype=jnp.int32) * UP + jnp.arange(UP, dtype=jnp.int32)
    order = jnp.argsort(scores, axis=2)[:, :, :CAP].astype(jnp.int32)
    offsets = lax.broadcasted_iota(jnp.int32, (devices_count, NOFF, CAP), 1)
    keep = (jax.random.randint(second, (devices_count, NOFF, CAP), 0, 5, dtype=jnp.int32) < 3) | (offsets == REACH)
    return jnp.where(keep, order, -1).astype(jnp.int32)


def draw_cross_pair(key, part):
    first, second = jax.random.split(key)
    scores = jax.random.randint(first, (TILES_ALL, SLOTS), 0, 1 << 20, dtype=jnp.int32) * SLOTS + jnp.arange(SLOTS, dtype=jnp.int32)
    order = jnp.argsort(scores, axis=1)[:, :NC].astype(jnp.int32)
    keep = jax.random.randint(second, (TILES_ALL, NC), 0, 4, dtype=jnp.int32) != 0
    return jnp.where(keep, order, -1).astype(jnp.int32)


def touch_ends(drawn, stream_key, low, high):
    spot = [jax.random.randint(jax.random.fold_in(stream_key, axis), (), 0, length) for axis, length in enumerate(drawn.shape)]
    widest = drawn.shape.index(max(drawn.shape))
    beside = spot[:widest] + [(spot[widest] + 1) % drawn.shape[widest]] + spot[widest + 1:]
    return drawn.at[tuple(spot)].set(low).at[tuple(beside)].set(high)


def levels(rng, dims, cuts, smallest, high):
    def one(axis_at, blocks):
        draws = jax.random.uniform(jax.random.fold_in(jax.random.fold_in(rng, 6), axis_at), (blocks,), jnp.float32, smallest / len(cuts), high / len(cuts))
        return jnp.repeat(jnp.exp(draws), dims[axis_at] // blocks).reshape((-1,) + (1,) * (len(dims) - axis_at - 1))

    level = one(*cuts[0])
    for cut in cuts[1:]:
        level = level * one(*cut)
    return level


def gaussian(rng, dims, width, reach, cuts=(), kind=jnp.bfloat16):
    level = levels(rng, dims, cuts, -0.22, 0.18) if cuts else 1.0
    entries = jax.random.normal(rng, dims, jnp.float32) * width * level
    return jnp.minimum(jnp.maximum(entries, -reach), reach).astype(kind)


def setup_inputs(seed: int = 0) -> dict:
    keys = jax.random.split(jax.random.key(seed), 10)
    positions = jnp.clip(6.0 * jax.random.uniform(keys[0], (3, BEADS), jnp.float32) ** levels(keys[0], (3, BEADS), ((1, 32),), -0.2, 0.2), 0.0, 6.0)
    velocities = gaussian(keys[1], (3, BEADS), 1.0, 6.0, ((1, 32),), jnp.float32)
    types = touch_ends(jax.random.randint(keys[2], (BEADS,), 0, NTYPE), jax.random.fold_in(keys[2], 1), 0, NTYPE - 1).astype(jnp.int32)
    counts = draw_counts(jax.random.fold_in(keys[9], 71), 0)
    a_table = jnp.clip(jax.random.uniform(keys[4], (NTYPE, NTYPE), jnp.float32, -60.0, -20.0), -60.0, -20.0)
    local_nbr = draw_local_nbr(jax.random.fold_in(keys[9], 71), 0)
    face_nbr = draw_face_nbr(jax.random.fold_in(keys[9], 71), 0)
    cross_send = draw_cross_send(jax.random.fold_in(keys[9], 71), 0)
    cross_pair = draw_cross_pair(jax.random.fold_in(keys[9], 71), 0)
    return {"positions": positions, "velocities": velocities, "types": types, "counts": counts, "a_table": a_table, "local_nbr": local_nbr, "face_nbr": face_nbr, "cross_send": cross_send, "cross_pair": cross_pair}


cutoff_force = 1.0
cutoff_density = 0.75
density_norm = 15.0 / (2.0 * math.pi * cutoff_density ** 3)
repulse = 25.0
friction = 4.5
time_step = 0.01
distance_floor = 0.01

def geometry(place_left, place_right):
    between = place_left[:, :, :, None] - place_right[:, :, None, :]
    distance = jnp.sqrt(jnp.maximum(lax.optimization_barrier(jnp.sum(between * between, axis=1)), distance_floor))
    return (between, distance)

def ordered_pairs(extent):
    rows_index = lax.broadcasted_iota(jnp.int32, (extent, extent), 0)
    cols_index = lax.broadcasted_iota(jnp.int32, (extent, extent), 1)
    return (rows_index < cols_index).astype(jnp.float32)

def density_terms(place_left, alive_left, place_right, alive_right, within):
    between, distance = geometry(place_left, place_right)
    weight = alive_left[:, :, None] * alive_right[:, None, :]
    if within:
        weight = weight * ordered_pairs(distance.shape[-1])[None]
    reach_term = jnp.maximum(1.0 - distance / cutoff_density, 0.0)
    weight = weight * density_norm * reach_term * reach_term
    return (lax.optimization_barrier(jnp.sum(weight, axis=2)), lax.optimization_barrier(jnp.sum(weight, axis=1)))

def force_terms(place_left, speed_left, density_left, species_left, alive_left, place_right, speed_right, density_right, strength_right, alive_right, within):
    between, distance = geometry(place_left, place_right)
    weight = alive_left[:, :, None] * alive_right[:, None, :]
    if within:
        weight = weight * ordered_pairs(distance.shape[-1])[None]
    conserve = jnp.maximum(1.0 - distance / cutoff_force, 0.0)
    crowding = jnp.maximum(1.0 - distance / cutoff_density, 0.0)
    amplitude = lax.optimization_barrier(jnp.sum(species_left[:, :, :, None] * strength_right[:, :, None, :], axis=1))
    relative = speed_left[:, :, :, None] - speed_right[:, :, None, :]
    approach = lax.optimization_barrier(jnp.sum(between * relative, axis=1)) / distance
    scalar = amplitude * conserve + repulse * (density_left[:, :, None] + density_right[:, None, :]) * crowding
    scalar = scalar - friction * conserve * conserve * approach
    scalar = scalar * weight / distance
    pushed = between * scalar[:, None]
    return (lax.optimization_barrier(jnp.sum(pushed, axis=3)), -lax.optimization_barrier(jnp.sum(pushed, axis=2)))

def blocked_map(kernel, inputs):
    extent = inputs[0].shape[0]
    size_block = math.gcd(extent, 64)
    shaped = tuple((element.reshape((extent // size_block, size_block) + element.shape[1:]) for element in inputs))
    results = lax.map(lambda group: kernel(*group), shaped)
    return tuple((element.reshape((extent,) + element.shape[2:]) for element in results))

def reference(positions, velocities, types, counts, a_table, local_nbr, face_nbr, cross_send, cross_pair):
    place = positions.reshape(3, TILES_ALL, TILE).transpose(1, 0, 2)
    speed = velocities.reshape(3, TILES_ALL, TILE).transpose(1, 0, 2)
    kinds_grid = types.reshape(TILES_ALL, TILE)
    species = (kinds_grid[:, None, :] == jnp.arange(NTYPE, dtype=jnp.int32)[None, :, None]).astype(jnp.float32)
    within_tile = lax.broadcasted_iota(jnp.int32, (TILES_ALL, TILE), 1)
    alive = (within_tile < counts[:, None]).astype(jnp.float32)
    symmetric = 0.5 * (a_table + a_table.T)
    strength = jnp.einsum('km,tmi->tki', symmetric, species, precision=lax.Precision.HIGHEST)
    tile_index = jnp.arange(TILES_ALL, dtype=jnp.int32)
    device = tile_index // TILES_DEV
    layer_place = device // N_LAT
    lateral = device % N_LAT
    columns = [(tile_index, jnp.ones((TILES_ALL,), jnp.bool_), True)]
    for column in range(NL):
        entry = local_nbr[:, column]
        columns.append((device * TILES_DEV + jnp.maximum(entry, 0), entry >= 0, False))
    lower_device = layer_place * N_LAT + (lateral - 1) % N_LAT
    for column in range(NF):
        entry = face_nbr[:, column]
        columns.append((lower_device * TILES_DEV + jnp.maximum(entry, 0), entry >= 0, False))
    for column in range(NC):
        entry = cross_pair[:, column]
        clipped = jnp.maximum(entry, 0)
        offset = clipped // CAP
        within_offset = clipped % CAP
        source = (layer_place - 1) * N_LAT + (lateral - offset + REACH) % N_LAT
        source = jnp.maximum(source, 0)
        offered = cross_send[source, offset, within_offset]
        valid = (entry >= 0) & (layer_place >= 1) & (offered >= 0)
        partner = source * TILES_DEV + TILES_DEV - UP + jnp.maximum(offered, 0)
        columns.append((partner.astype(jnp.int32), valid, False))
    density = jnp.zeros((TILES_ALL, TILE), jnp.float32)
    for partner, valid, within in columns:
        right_alive = jnp.take(alive, partner, axis=0) * valid.astype(jnp.float32)[:, None]
        rows_sum, cols_sum = blocked_map(functools.partial(density_terms, within=within), (place, alive, jnp.take(place, partner, axis=0), right_alive))
        density = density + rows_sum
        density = density.at[partner].add(cols_sum)
    force = jnp.zeros((TILES_ALL, 3, TILE), jnp.float32)
    for partner, valid, within in columns:
        right_alive = jnp.take(alive, partner, axis=0) * valid.astype(jnp.float32)[:, None]
        rows_sum, cols_sum = blocked_map(functools.partial(force_terms, within=within), (place, speed, density, species, alive, jnp.take(place, partner, axis=0), jnp.take(speed, partner, axis=0), jnp.take(density, partner, axis=0), jnp.take(strength, partner, axis=0), right_alive))
        force = force + rows_sum
        force = force.at[partner].add(cols_sum)
    speed_next = (speed + time_step * force) * alive[:, None, :]
    place_next = (place + time_step * speed_next) * alive[:, None, :]
    new_positions = place_next.transpose(1, 0, 2).reshape(3, BEADS)
    new_velocities = speed_next.transpose(1, 0, 2).reshape(3, BEADS)
    return (new_positions, new_velocities)
```

```python
import functools
import math

import jax
import jax.numpy as jnp
from jax import lax
from jax.experimental import pallas as pl
from jax.experimental.pallas import tpu as pltpu
from jax.sharding import PartitionSpec as P

cutoff_density = 0.75
density_norm = 15.0 / (2.0 * math.pi * cutoff_density**3)
repulse = 25.0
friction = 4.5
time_step = 0.01
distance_floor = 0.01
far_away = 10000.0
density_scale = density_norm / (cutoff_density * cutoff_density)
crowd_scale = repulse / cutoff_density
STEP = 16
VMEM = pl.BlockSpec(memory_space=pltpu.VMEM)
SMEM = pl.BlockSpec(memory_space=pltpu.SMEM)
f32 = jnp.float32


def sds(*shape):
    return jax.ShapeDtypeStruct(shape, f32)


def params():
    return pltpu.CompilerParams(vmem_limit_bytes=32 * 1024 * 1024)


def pack_kernel(pos, vel, typ, counts, send, out, top, face):
    tiles = out.shape[0]
    width = out.shape[2]
    lane = lax.broadcasted_iota(jnp.int32, (1, width), 1)
    upper = top.shape[0]
    offsets, cap = send.shape[1], send.shape[2]
    for g in range(tiles):
        cols = pl.ds(g * width, width)
        live = lane < counts[g]
        for c in range(3):
            out[g, pl.ds(c, 1), :] = jnp.where(live, pos[pl.ds(c, 1), cols], far_away)
            out[g, pl.ds(3 + c, 1), :] = vel[pl.ds(c, 1), cols]
        out[g, pl.ds(6, 1), :] = typ[pl.ds(g, 1), :].astype(f32)
        meta = jnp.full((1, width), counts[g], jnp.int32)
        o = g - (tiles - upper)
        if 0 <= o < offsets:
            for c in range(cap):
                meta = jnp.where(lane == c, send[0, o, c], meta)
        out[g, pl.ds(7, 1), :] = meta.astype(f32)
    top[...] = out[pl.ds(tiles - upper, upper)]
    face[...] = out[pl.ds(0, face.shape[0])]


def spread_rows(tile, rows, channels):
    width = tile.shape[1]
    turned = tile.T
    for c in range(channels):
        rows[c] = jnp.broadcast_to(turned[:, c : c + 1], (width, width))


def sized(count, width, body):
    steps = (count + (STEP - 1)) // STEP

    def case(k):
        @pl.when(steps == k)
        def _():
            body(k * STEP)

    for k in range(1, width // STEP + 1):
        case(k)


def density_block(rows, other, r):
    at = pl.ds(r, 8)
    dx = rows[0, at, :] - other[0]
    dy = rows[1, at, :] - other[1]
    dz = rows[2, at, :] - other[2]
    d2 = jnp.maximum(dx * dx + dy * dy + dz * dz, distance_floor)
    w = jnp.maximum(cutoff_density - d2 * lax.rsqrt(d2), 0.0)
    return w * w


def column(ref, h, c):
    return jnp.broadcast_to(ref[h, pl.ds(c, 1), :], (8, ref.shape[2]))


def density_pair(rows, union, h, count, acc_cols, acc_rows):
    width = union.shape[2]

    def body(n):
        other = [column(union, h, c) for c in range(3)]
        total = None
        for r in range(0, n, 8):
            w = density_block(rows, other, r)
            total = w if total is None else total + w
            if acc_rows is not None:
                acc_rows[0, pl.ds(r, 8), :] += w
        acc_cols[h] += total

    sized(count, width, body)


def force_pair(rows, union, h, count, table, acc_cols, acc_rows):
    width = union.shape[2]
    a00, a01, a11 = table

    def body(n):
        other = [column(union, h, c) for c in range(8)]
        first = a00 + other[6] * (a01 - a00)
        slope = (a01 + other[6] * (a11 - a01)) - first
        total = [None] * 3
        for r in range(0, n, 8):
            mine = [rows[c, pl.ds(r, 8), :] for c in range(8)]
            d = [mine[c] - other[c] for c in range(3)]
            d2 = jnp.maximum(d[0] * d[0] + d[1] * d[1] + d[2] * d[2], distance_floor)
            inverse = lax.rsqrt(d2)
            dist = d2 * inverse
            wc = jnp.maximum(1.0 - dist, 0.0)
            wd = jnp.maximum(cutoff_density - dist, 0.0)
            dv = [mine[3 + c] - other[3 + c] for c in range(3)]
            approach = (d[0] * dv[0] + d[1] * dv[1] + d[2] * dv[2]) * inverse
            scalar = (first + mine[6] * slope) - approach * wc
            scalar = scalar * wc + (mine[7] + other[7]) * wd
            scalar = scalar * inverse
            for c in range(3):
                push = d[c] * scalar
                total[c] = push if total[c] is None else total[c] + push
                if acc_rows is not None:
                    acc_rows[c, pl.ds(r, 8), :] += push
        for c in range(3):
            acc_cols[c, h] -= total[c]

    sized(count, width, body)


def row_sums(acc):
    first = (lax.broadcasted_iota(jnp.int32, (8, acc.shape[1]), 0) == 0).astype(f32)
    return lax.dot_general(
        first,
        acc,
        (((1,), (1,)), ((), ())),
        precision=lax.Precision.HIGHEST,
        preferred_element_type=f32,
    )


def fold(ref, tiles, out, scale=None):
    def one(t, carry):
        value = jnp.sum(ref[t], axis=0, keepdims=True)
        out[pl.ds(t, 1), :] = value
        return carry

    lax.fori_loop(0, tiles, one, 0)


def local_density_kernel(counts, nbr, union, acc, rows, acc_rows):
    tiles, width = union.shape[0], union.shape[2]
    acc[...] = jnp.zeros_like(acc)

    def tile(g, carry):
        count = counts[g]

        @pl.when(count > 0)
        def _():
            spread_rows(union[g], rows, 3)
            density_pair(rows, union, g, count, acc, None)
            acc_rows[0] = jnp.zeros((width, width), f32)

            def partner(k, carry):
                h = nbr[g, k]

                @pl.when((h >= 0) & (counts[jnp.maximum(h, 0)] > 0))
                def _():
                    density_pair(rows, union, h, count, acc, acc_rows)

                return carry

            lax.fori_loop(0, nbr.shape[1], partner, 0)
            acc[g] += row_sums(acc_rows[0])

        return carry

    lax.fori_loop(0, tiles, tile, 0)


def gather_ghosts(ghosts, face, near, flip, below, above):
    at = 0
    for ref in (face, near, flip, below, above):
        ghosts[pl.ds(at, ref.shape[0])] = ref[...]
        at += ref.shape[0]


def ghost_meta(ghosts, faces, upper, meta, meta_smem, sem):
    total = ghosts.shape[0]
    for t in range(total):
        meta[pl.ds(t, 1), :] = ghosts[t, pl.ds(7, 1), :].astype(jnp.int32)
    copy = pltpu.make_async_copy(meta, meta_smem, sem)
    copy.start()
    copy.wait()


def ghost_partner(k, g, face_nbr, cross_pair, where, meta, faces, upper, cap, reach):
    columns = face_nbr.shape[1]
    is_face = k < columns
    f = face_nbr[g, jnp.minimum(k, columns - 1)]
    s = cross_pair[g, jnp.maximum(k - columns, 0)]
    layer, core = where[0], where[1]
    slot = jnp.maximum(s, 0)
    o = slot // cap
    c = slot - o * cap
    place = core - o + 2 * reach
    hop = place // 2 - 1
    flipped = jnp.where(lax.rem(place, 2) == core, 0, 1)
    hops = jnp.where(hop == 0, 0, jnp.where(hop < 0, 1, 2))
    base = faces + (hops * 2 + flipped) * upper
    u = meta[base + o, c]
    ok = (s >= 0) & (layer > 0) & (u >= 0)
    h = jnp.where(is_face, jnp.maximum(f, 0), base + jnp.maximum(u, 0))
    ok = jnp.where(is_face, f >= 0, ok)
    return h, ok & (meta[h, meta.shape[1] - 1] > 0)


def ghost_density_kernel(
    faces,
    upper,
    cap,
    reach,
    where,
    counts,
    face_nbr,
    cross_pair,
    union,
    local_acc,
    face,
    near,
    flip,
    below,
    above,
    own_out,
    top_out,
    face_out,
    pair_out,
    below_out,
    above_out,
    ghosts,
    acc,
    acc_own,
    rows,
    acc_rows,
    reduced,
    meta,
    meta_smem,
    sem,
):
    tiles, width = union.shape[0], union.shape[2]
    gather_ghosts(ghosts, face, near, flip, below, above)
    ghost_meta(ghosts, faces, upper, meta, meta_smem, sem)
    acc[...] = jnp.zeros_like(acc)
    columns = face_nbr.shape[1] + cross_pair.shape[1]

    def tile(g, carry):
        count = counts[g]
        acc_own[g] = local_acc[g]

        @pl.when(count > 0)
        def _():
            spread_rows(union[g], rows, 3)
            acc_rows[0] = jnp.zeros((width, width), f32)

            def partner(k, carry):
                h, ok = ghost_partner(
                    k, g, face_nbr, cross_pair, where, meta_smem, faces, upper, cap, reach
                )

                @pl.when(ok)
                def _():
                    density_pair(rows, ghosts, h, count, acc, acc_rows)

                return carry

            lax.fori_loop(0, columns, partner, 0)
            acc_own[g] += row_sums(acc_rows[0])

        return carry

    lax.fori_loop(0, tiles, tile, 0)
    self_term = (cutoff_density - math.sqrt(distance_floor)) ** 2
    for t in range(tiles):
        lane = lax.broadcasted_iota(jnp.int32, (1, width), 1)
        value = jnp.sum(acc_own[t], axis=0, keepdims=True)
        own_out[pl.ds(t, 1), :] = value - jnp.where(lane < counts[t], self_term, 0.0)
    top_out[...] = own_out[pl.ds(tiles - upper, upper)]
    for t in range(acc.shape[0]):
        reduced[pl.ds(t, 1), :] = jnp.sum(acc[t], axis=0, keepdims=True)
    face_out[...] = reduced[pl.ds(0, faces)]
    pair_out[...] = reduced[pl.ds(faces, 2 * upper)]
    below_out[...] = reduced[pl.ds(faces + 2 * upper, 2 * upper)]
    above_out[...] = reduced[pl.ds(faces + 4 * upper, 2 * upper)]


def force_tile(union, density, t):
    tile = union[t]
    channel = lax.broadcasted_iota(jnp.int32, tile.shape, 0)
    tile = jnp.where((channel >= 3) & (channel < 6), tile * friction, tile)
    return jnp.where(channel == 7, density * (crowd_scale * density_scale), tile)


def amplitudes(a_table):
    return (a_table[0, 0], 0.5 * (a_table[0, 1] + a_table[1, 0]), a_table[1, 1])


def local_force_kernel(counts, nbr, a_table, union, density, acc, beads, rows, acc_rows):
    tiles, width = union.shape[0], union.shape[2]
    table = amplitudes(a_table)
    acc[...] = jnp.zeros_like(acc)
    for t in range(tiles):
        beads[t] = force_tile(union, density[pl.ds(t, 1), :], t)

    def tile(g, carry):
        count = counts[g]

        @pl.when(count > 0)
        def _():
            spread_rows(beads[g], rows, 8)
            force_pair(rows, beads, g, count, table, acc, None)
            acc_rows[...] = jnp.zeros_like(acc_rows)

            def partner(k, carry):
                h = nbr[g, k]

                @pl.when((h >= 0) & (counts[jnp.maximum(h, 0)] > 0))
                def _():
                    force_pair(rows, beads, h, count, table, acc, acc_rows)

                return carry

            lax.fori_loop(0, nbr.shape[1], partner, 0)
            for c in range(3):
                acc[c, g] += row_sums(acc_rows[c])

        return carry

    lax.fori_loop(0, tiles, tile, 0)


def ghost_force_kernel(
    faces,
    upper,
    cap,
    reach,
    where,
    counts,
    face_nbr,
    cross_pair,
    a_table,
    union,
    density,
    face,
    near,
    flip,
    below,
    above,
    face_rho,
    pair_rho,
    below_rho,
    above_rho,
    own_out,
    face_out,
    pair_out,
    below_out,
    above_out,
    ghosts,
    beads,
    acc,
    rho,
    rows,
    acc_rows,
    reduced,
    meta,
    meta_smem,
    sem,
):
    tiles, width = union.shape[0], union.shape[2]
    gather_ghosts(ghosts, face, near, flip, below, above)
    ghost_meta(ghosts, faces, upper, meta, meta_smem, sem)
    acc[...] = jnp.zeros_like(acc)
    own_out[...] = jnp.zeros_like(own_out)
    table = amplitudes(a_table)
    columns = face_nbr.shape[1] + cross_pair.shape[1]
    at = 0
    for ref in (face_rho, pair_rho, below_rho, above_rho):
        rho[pl.ds(at, ref.shape[0]), :] = ref[...]
        at += ref.shape[0]
    for t in range(ghosts.shape[0]):
        ghosts[t] = force_tile(ghosts, rho[pl.ds(t, 1), :], t)
    for t in range(tiles):
        beads[t] = force_tile(union, density[pl.ds(t, 1), :], t)

    def tile(g, carry):
        count = counts[g]

        @pl.when(count > 0)
        def _():
            spread_rows(beads[g], rows, 8)
            acc_rows[...] = jnp.zeros_like(acc_rows)

            def partner(k, carry):
                h, ok = ghost_partner(
                    k, g, face_nbr, cross_pair, where, meta_smem, faces, upper, cap, reach
                )

                @pl.when(ok)
                def _():
                    force_pair(rows, ghosts, h, count, table, acc, acc_rows)

                return carry

            lax.fori_loop(0, columns, partner, 0)
            for c in range(3):
                own_out[c, g] = row_sums(acc_rows[c])

        return carry

    lax.fori_loop(0, tiles, tile, 0)
    for c in range(3):
        for t in range(acc.shape[1]):
            reduced[pl.ds(t, 1), :] = jnp.sum(acc[c, t], axis=0, keepdims=True)
        face_out[c] = reduced[pl.ds(0, faces)]
        pair_out[c] = reduced[pl.ds(faces, 2 * upper)]
        below_out[c] = reduced[pl.ds(faces + 2 * upper, 2 * upper)]
        above_out[c] = reduced[pl.ds(faces + 4 * upper, 2 * upper)]


def finish_kernel(counts, pos, vel, local_acc, ghost_acc, face_back, top_back, pos_out, vel_out):
    tiles, width = local_acc.shape[1], local_acc.shape[3]
    faces, upper = face_back.shape[1], top_back.shape[1]
    lane = lax.broadcasted_iota(jnp.int32, (1, width), 1)
    for g in range(tiles):
        cols = pl.ds(g * width, width)
        live = lane < counts[g]
        for c in range(3):
            force = jnp.sum(local_acc[c, g] + ghost_acc[c, g], axis=0, keepdims=True)
            if g < faces:
                force = force + face_back[c, pl.ds(g, 1), :]
            if g >= tiles - upper:
                force = force + top_back[c, pl.ds(g - (tiles - upper), 1), :]
            speed = jnp.where(live, vel[pl.ds(c, 1), cols] + time_step * force, 0.0)
            vel_out[pl.ds(c, 1), cols] = speed
            place = jnp.where(live, pos[pl.ds(c, 1), cols] + time_step * speed, 0.0)
            pos_out[pl.ds(c, 1), cols] = place


def on_device(
    layers,
    places,
    positions,
    velocities,
    types,
    counts,
    a_table,
    local_nbr,
    face_nbr,
    cross_send,
    cross_pair,
):
    tiles = counts.shape[0]
    width = positions.shape[1] // tiles
    faces, upper = tiles // 4, tiles // 2
    offsets, cap = cross_send.shape[1], cross_send.shape[2]
    reach = offsets // 2
    total = faces + 6 * upper
    both = ("layer", "lat")

    def lateral(value, by):
        return lax.ppermute(value, "lat", [(m, (m + by) % places) for m in range(places)])

    def swap(value):
        return lax.ppermute(value, "lat", [(m, m ^ 1) for m in range(places)])

    def climb(value, by, flip=0):
        return lax.ppermute(
            value,
            both,
            [
                (l * places + m, ((l + by) % layers) * places + (m ^ flip))
                for l in range(layers)
                for m in range(places)
            ],
        )

    kinds = types.reshape(tiles, width)
    payload, top, face = pl.pallas_call(
        pack_kernel,
        out_shape=(sds(tiles, 8, width), sds(upper, 8, width), sds(faces, 8, width)),
        in_specs=[VMEM, VMEM, VMEM, SMEM, SMEM],
        out_specs=[VMEM] * 3,
        compiler_params=params(),
    )(positions, velocities, kinds, counts, cross_send)
    near = climb(top, 1)
    flip = climb(top, 1, 1)
    face_ghosts = lateral(face, 1)
    chip_ghosts = jnp.concatenate([near, flip], axis=0)
    below = lateral(chip_ghosts, 2)
    above = lateral(chip_ghosts, -2)
    where = jnp.stack([lax.axis_index("layer"), lax.axis_index("lat") % 2]).astype(jnp.int32)

    local_acc = pl.pallas_call(
        local_density_kernel,
        out_shape=sds(tiles, 8, width),
        in_specs=[SMEM, SMEM, VMEM],
        out_specs=VMEM,
        scratch_shapes=[pltpu.VMEM((3, width, width), f32), pltpu.VMEM((1, width, width), f32)],
        cost_estimate=pl.CostEstimate(flops=200 * 10**6, bytes_accessed=10**6, transcendentals=0),
        compiler_params=params(),
    )(counts, local_nbr, payload)

    sizes = (faces, upper, cap, reach)
    meta_scratch = [
        pltpu.VMEM((total, width), jnp.int32),
        pltpu.SMEM((total, width), jnp.int32),
        pltpu.SemaphoreType.DMA,
    ]
    own, own_top, face_part, pair_part, below_part, above_part = pl.pallas_call(
        functools.partial(ghost_density_kernel, *sizes),
        out_shape=(
            sds(tiles, width),
            sds(upper, width),
            sds(faces, width),
            sds(2 * upper, width),
            sds(2 * upper, width),
            sds(2 * upper, width),
        ),
        in_specs=[SMEM] * 4 + [VMEM] * 7,
        out_specs=[VMEM] * 6,
        scratch_shapes=[
            pltpu.VMEM((total, 8, width), f32),
            pltpu.VMEM((total, 8, width), f32),
            pltpu.VMEM((tiles, 8, width), f32),
            pltpu.VMEM((3, width, width), f32),
            pltpu.VMEM((1, width, width), f32),
            pltpu.VMEM((total, width), f32),
        ]
        + meta_scratch,
        compiler_params=params(),
    )(
        where,
        counts,
        face_nbr,
        cross_pair,
        payload,
        local_acc,
        face_ghosts,
        near,
        flip,
        below,
        above,
    )

    owner_part = climb(own_top, 1)
    from_above = lateral(below_part, -2)
    from_below = lateral(above_part, 2)
    face_back = lateral(face_part, -1)
    met = pair_part + from_above + from_below
    met = jnp.concatenate([met[:upper] + owner_part, met[upper:]], axis=0)
    other = swap(met)
    pair_rho = met + jnp.concatenate([other[upper:], other[:upper]], axis=0)
    top_rho = climb(pair_rho[:upper], -1)
    below_rho = lateral(pair_rho, 2)
    above_rho = lateral(pair_rho, -2)
    bottom_rho = own[:faces] + face_back
    face_rho = lateral(bottom_rho, 1)
    density = jnp.concatenate([bottom_rho, own[faces : tiles - upper], top_rho], axis=0)

    ghost_acc, face_force, pair_force, below_force, above_force = pl.pallas_call(
        functools.partial(ghost_force_kernel, *sizes),
        out_shape=(
            sds(3, tiles, 8, width),
            sds(3, faces, width),
            sds(3, 2 * upper, width),
            sds(3, 2 * upper, width),
            sds(3, 2 * upper, width),
        ),
        in_specs=[SMEM] * 5 + [VMEM] * 11,
        out_specs=[VMEM] * 5,
        scratch_shapes=[
            pltpu.VMEM((total, 8, width), f32),
            pltpu.VMEM((tiles, 8, width), f32),
            pltpu.VMEM((3, total, 8, width), f32),
            pltpu.VMEM((total, width), f32),
            pltpu.VMEM((8, width, width), f32),
            pltpu.VMEM((3, width, width), f32),
            pltpu.VMEM((total, width), f32),
        ]
        + meta_scratch,
        compiler_params=params(),
    )(
        where,
        counts,
        face_nbr,
        cross_pair,
        a_table,
        payload,
        density,
        face_ghosts,
        near,
        flip,
        below,
        above,
        face_rho,
        pair_rho,
        below_rho,
        above_rho,
    )

    force_face = lateral(face_force, -1)
    force_met = pair_force + lateral(below_force, -2) + lateral(above_force, 2)
    force_other = swap(force_met[:, upper:])
    force_top = climb(force_met[:, :upper] + force_other, -1)

    local_force = pl.pallas_call(
        local_force_kernel,
        out_shape=sds(3, tiles, 8, width),
        in_specs=[SMEM, SMEM, SMEM, VMEM, VMEM],
        out_specs=VMEM,
        scratch_shapes=[
            pltpu.VMEM((tiles, 8, width), f32),
            pltpu.VMEM((8, width, width), f32),
            pltpu.VMEM((3, width, width), f32),
        ],
        cost_estimate=pl.CostEstimate(flops=400 * 10**6, bytes_accessed=10**6, transcendentals=0),
        compiler_params=params(),
    )(counts, local_nbr, a_table, payload, density)

    return pl.pallas_call(
        finish_kernel,
        out_shape=(sds(*positions.shape), sds(*velocities.shape)),
        in_specs=[SMEM] + [VMEM] * 6,
        out_specs=[VMEM] * 2,
        compiler_params=params(),
    )(counts, positions, velocities, local_force, ghost_acc, force_face, force_top)


def solution(mesh):
    placed = (
        P(None, ("layer", "lat")),
        P(None, ("layer", "lat")),
        P(("layer", "lat")),
        P(("layer", "lat")),
        P(),
        P(("layer", "lat"), None),
        P(("layer", "lat"), None),
        P(("layer", "lat"), None, None),
        P(("layer", "lat"), None),
    )
    return jax.shard_map(
        functools.partial(on_device, mesh.shape["layer"], mesh.shape["lat"]),
        mesh=mesh,
        in_specs=placed,
        out_specs=(P(None, ("layer", "lat")), P(None, ("layer", "lat"))),
        check_vma=False,
    )
```

```python
import functools
import math

import jax
import jax.numpy as jnp
from jax import lax
from jax.experimental import pallas as pl
from jax.experimental.pallas import tpu as pltpu
from jax.sharding import PartitionSpec as P

cutoff_density = 0.75
density_norm = 15.0 / (2.0 * math.pi * cutoff_density**3)
repulse = 25.0
friction = 4.5
time_step = 0.01
distance_floor = 0.01
far_away = 10000.0
density_scale = density_norm / (cutoff_density * cutoff_density)
crowd_scale = repulse / cutoff_density
VMEM = pl.BlockSpec(memory_space=pltpu.VMEM)
SMEM = pl.BlockSpec(memory_space=pltpu.SMEM)
f32 = jnp.float32


def sds(*shape):
    return jax.ShapeDtypeStruct(shape, f32)


def params():
    return pltpu.CompilerParams(vmem_limit_bytes=32 * 1024 * 1024)


def pack_kernel(pos, vel, typ, counts, send, out, top, face):
    tiles = out.shape[0]
    width = out.shape[2]
    lane = lax.broadcasted_iota(jnp.int32, (1, width), 1)
    upper = top.shape[0]
    offsets, cap = send.shape[1], send.shape[2]
    for g in range(tiles):
        cols = pl.ds(g * width, width)
        live = lane < counts[g]
        for c in range(3):
            out[g, pl.ds(c, 1), :] = jnp.where(live, pos[pl.ds(c, 1), cols], far_away)
            out[g, pl.ds(3 + c, 1), :] = vel[pl.ds(c, 1), cols]
        out[g, pl.ds(6, 1), :] = typ[pl.ds(g, 1), :].astype(f32)
        meta = jnp.full((1, width), counts[g], jnp.int32)
        o = g - (tiles - upper)
        if 0 <= o < offsets:
            for c in range(cap):
                meta = jnp.where(lane == c, send[0, o, c], meta)
        out[g, pl.ds(7, 1), :] = meta.astype(f32)
    top[...] = out[pl.ds(tiles - upper, upper)]
    face[...] = out[pl.ds(0, face.shape[0])]


def diagonal(width):
    lane = lax.broadcasted_iota(jnp.int32, (8, width), 1)
    return lane - lax.broadcasted_iota(jnp.int32, (8, width), 0)


def spread_row(row, store):
    width = row.shape[1]
    diff = diagonal(width)
    row = jnp.broadcast_to(row, (8, width))
    for r in range(0, width, 8):
        one = jnp.sum(jnp.where(diff == r, row, 0.0), axis=1, keepdims=True)
        store(r, jnp.broadcast_to(one, (8, width)))


def row_sums(acc, c):
    width = acc.shape[2]
    diff = diagonal(width)
    out = jnp.zeros((8, width), f32)
    for r in range(0, width, 8):
        out = jnp.where(diff == r, jnp.sum(acc[c, pl.ds(r, 8), :], axis=1, keepdims=True), out)
        acc[c, pl.ds(r, 8), :] = jnp.zeros((8, width), f32)
    return out


def branch(used, count, width, body):
    sizes = (0,) + tuple(width * e // 8 for e in (4, 6, 8))
    index = jnp.where(used, 1, 0)
    for n in sizes[1:-1]:
        index += jnp.where(used & (count > n), 1, 0)

    def pick(low, high):
        if low == high:
            body(sizes[low])
            return
        middle = (low + high) // 2

        @pl.when(index <= middle)
        def _():
            pick(low, middle)

        @pl.when(index > middle)
        def _():
            pick(middle + 1, high)

    pick(0, len(sizes) - 1)


def tile_loop(tiles, width, counts, slots, partner, pair, tasks):
    def step(i, carry):
        for half in range(2):
            g = 2 * i + half
            count = counts[g]
            work = tasks(g, half)
            for k in range(slots):
                h, used = partner(g, k)

                def body(n, k=k, h=h):
                    if n:
                        pair(g, half, k, h, n)
                    for task in work[k::slots]:
                        task()

                branch(used & (count > 0), count, width, body)
        return carry

    lax.fori_loop(0, tiles // 2, step, 0)


def column(ref, h, c):
    return jnp.broadcast_to(ref[h, pl.ds(c, 1), :], (8, ref.shape[2]))


def density_pair(mine, union, h, n, acc_cols, acc_rows):
    other = [column(union, h, c) for c in range(3)]
    total = None
    for r in range(0, n, 8):
        d = [mine(c, r) - other[c] for c in range(3)]
        d2 = jnp.maximum(d[0] * d[0] + d[1] * d[1] + d[2] * d[2], distance_floor)
        w = jnp.maximum(cutoff_density - d2 * lax.rsqrt(d2), 0.0)
        w = w * w
        total = w if total is None else total + w
        if acc_rows is not None:
            acc_rows[0, pl.ds(r, 8), :] += w
    acc_cols[h] += total


def force_pair(mine, union, h, n, table, acc_cols, acc_rows):
    a00, a01, a11 = table
    other = [column(union, h, c) for c in range(8)]
    first = a00 + other[6] * (a01 - a00)
    slope = (a01 + other[6] * (a11 - a01)) - first
    total = [None] * 3
    for r in range(0, n, 8):
        d = [mine(c, r) - other[c] for c in range(3)]
        d2 = jnp.maximum(d[0] * d[0] + d[1] * d[1] + d[2] * d[2], distance_floor)
        inverse = lax.rsqrt(d2)
        dist = d2 * inverse
        wc = jnp.maximum(1.0 - dist, 0.0)
        wd = jnp.maximum(cutoff_density - dist, 0.0)
        dv = [mine(3 + c, r) - other[3 + c] for c in range(3)]
        approach = (d[0] * dv[0] + d[1] * dv[1] + d[2] * dv[2]) * inverse
        scalar = (first + mine(6, r) * slope) - approach * wc
        scalar = scalar * wc + (mine(7, r) + other[7]) * wd
        scalar = scalar * inverse
        for c in range(3):
            push = d[c] * scalar
            total[c] = push if total[c] is None else total[c] + push
            if acc_rows is not None:
                acc_rows[c, pl.ds(r, 8), :] += push
    for c in range(3):
        acc_cols[c, h] -= total[c]


def zero(*refs):
    for ref in refs:
        ref[...] = jnp.zeros_like(ref)


def local_density_kernel(counts, nbr, union, acc, spread, rows_0, rows_1, sums_0, sums_1):
    tiles, width = union.shape[0], union.shape[2]
    rows, sums = (rows_0, rows_1), (sums_0, sums_1)
    zero(acc, *sums)

    def fill(g, c, half):
        def store(r, value):
            spread[g, c, pl.ds(r, 8), :] = value
            if c < 3:
                rows[half][c, pl.ds(r, 8), :] = value

        row = union[g, pl.ds(c, 1), :]
        spread_row(row * friction if 3 <= c < 6 else row, store)

    def tasks(g, half):
        after, before = jnp.minimum(g + 1, tiles - 1), jnp.maximum(g - 1, 0)

        def collect():
            acc[before] += row_sums(sums[1 - half], 0)

        work = [functools.partial(fill, after, c, 1 - half) for c in range(spread.shape[1])]
        return work[:6] + [collect] + work[6:]

    def partner(g, k):
        if k == 0:
            return g, True
        h = nbr[g, k - 1]
        return jnp.maximum(h, 0), (h >= 0) & (counts[jnp.maximum(h, 0)] > 0)

    def pair(g, half, k, h, n):
        mine = lambda c, r: rows[half][c, pl.ds(r, 8), :]
        density_pair(mine, union, h, n, acc, sums[half] if k else None)

    for c in range(spread.shape[1]):
        fill(0, c, 0)
    tile_loop(tiles, width, counts, 1 + nbr.shape[1], partner, pair, tasks)
    acc[tiles - 1] += row_sums(sums[1], 0)


def gather_ghosts(ghosts, face, near, flip, below, above):
    at = 0
    for ref in (face, near, flip, below, above):
        ghosts[pl.ds(at, ref.shape[0])] = ref[...]
        at += ref.shape[0]


def ghost_meta(ghosts, faces, upper, meta, meta_smem, sem):
    total = ghosts.shape[0]
    for t in range(total):
        meta[pl.ds(t, 1), :] = ghosts[t, pl.ds(7, 1), :].astype(jnp.int32)
    copy = pltpu.make_async_copy(meta, meta_smem, sem)
    copy.start()
    copy.wait()


def ghost_partner(k, g, face_nbr, cross_pair, where, meta, faces, upper, cap, reach):
    columns = face_nbr.shape[1]
    if k < columns:
        f = face_nbr[g, k]
        h = jnp.maximum(f, 0)
        return h, (f >= 0) & (meta[h, meta.shape[1] - 1] > 0)
    s = cross_pair[g, k - columns]
    layer, core = where[0], where[1]
    slot = jnp.maximum(s, 0)
    o = slot // cap
    c = slot - o * cap
    place = core - o + 2 * reach
    hop = place // 2 - 1
    flipped = jnp.where(lax.rem(place, 2) == core, 0, 1)
    hops = jnp.where(hop == 0, 0, jnp.where(hop < 0, 1, 2))
    base = faces + (hops * 2 + flipped) * upper
    u = meta[base + o, c]
    h = base + jnp.maximum(u, 0)
    return h, (s >= 0) & (layer > 0) & (u >= 0) & (meta[h, meta.shape[1] - 1] > 0)


def ghost_density_kernel(
    faces,
    upper,
    cap,
    reach,
    where,
    counts,
    face_nbr,
    cross_pair,
    spread,
    local_acc,
    face,
    near,
    flip,
    below,
    above,
    own_out,
    top_out,
    face_out,
    pair_out,
    below_out,
    above_out,
    ghosts,
    acc,
    acc_own,
    sums_0,
    sums_1,
    reduced,
    meta,
    meta_smem,
    sem,
):
    tiles, width = spread.shape[0], spread.shape[2]
    sums = (sums_0, sums_1)
    gather_ghosts(ghosts, face, near, flip, below, above)
    ghost_meta(ghosts, faces, upper, meta, meta_smem, sem)
    zero(acc, *sums)
    acc_own[...] = local_acc[...]
    columns = face_nbr.shape[1] + cross_pair.shape[1]

    def tasks(g, half):
        before = jnp.maximum(g - 1, 0)

        def collect():
            acc_own[before] += row_sums(sums[1 - half], 0)

        return [collect]

    def partner(g, k):
        return ghost_partner(
            k, g, face_nbr, cross_pair, where, meta_smem, faces, upper, cap, reach
        )

    def pair(g, half, k, h, n):
        mine = lambda c, r: spread[g, c, pl.ds(r, 8), :]
        density_pair(mine, ghosts, h, n, acc, sums[half])

    tile_loop(tiles, width, counts, columns, partner, pair, tasks)
    acc_own[tiles - 1] += row_sums(sums[1], 0)
    self_term = (cutoff_density - math.sqrt(distance_floor)) ** 2
    for t in range(tiles):
        lane = lax.broadcasted_iota(jnp.int32, (1, width), 1)
        value = jnp.sum(acc_own[t], axis=0, keepdims=True)
        own_out[pl.ds(t, 1), :] = value - jnp.where(lane < counts[t], self_term, 0.0)
    top_out[...] = own_out[pl.ds(tiles - upper, upper)]
    for t in range(acc.shape[0]):
        reduced[pl.ds(t, 1), :] = jnp.sum(acc[t], axis=0, keepdims=True)
    face_out[...] = reduced[pl.ds(0, faces)]
    pair_out[...] = reduced[pl.ds(faces, 2 * upper)]
    below_out[...] = reduced[pl.ds(faces + 2 * upper, 2 * upper)]
    above_out[...] = reduced[pl.ds(faces + 4 * upper, 2 * upper)]


def force_tile(union, density, t):
    tile = union[t]
    channel = lax.broadcasted_iota(jnp.int32, tile.shape, 0)
    tile = jnp.where((channel >= 3) & (channel < 6), tile * friction, tile)
    return jnp.where(channel == 7, density * (crowd_scale * density_scale), tile)


def amplitudes(a_table):
    return (a_table[0, 0], 0.5 * (a_table[0, 1] + a_table[1, 0]), a_table[1, 1])


def force_tasks(tiles, beads, rows, sums, acc):
    def fill(g, half):
        def store(r, value):
            rows[half][pl.ds(r, 8), :] = value

        spread_row(beads[g, pl.ds(7, 1), :], store)

    def tasks(g, half):
        after, before = jnp.minimum(g + 1, tiles - 1), jnp.maximum(g - 1, 0)

        def collect(c):
            acc[c, before] += row_sums(sums[1 - half], c)

        work = [functools.partial(collect, c) for c in range(3)]
        return [functools.partial(fill, after, 1 - half)] + work

    def last():
        for c in range(3):
            acc[c, tiles - 1] += row_sums(sums[1], c)

    return lambda: fill(0, 0), tasks, last


def force_mine(spread, rows, g, half):
    def mine(c, r):
        return rows[half][pl.ds(r, 8), :] if c == 7 else spread[g, c, pl.ds(r, 8), :]

    return mine


def local_force_kernel(
    counts, nbr, a_table, union, spread, density, acc, beads, rows_0, rows_1, sums_0, sums_1
):
    tiles, width = union.shape[0], union.shape[2]
    rows, sums = (rows_0, rows_1), (sums_0, sums_1)
    table = amplitudes(a_table)
    zero(acc, *sums)
    for t in range(tiles):
        beads[t] = force_tile(union, density[pl.ds(t, 1), :], t)
    first, tasks, last = force_tasks(tiles, beads, rows, sums, acc)

    def partner(g, k):
        if k == 0:
            return g, True
        h = nbr[g, k - 1]
        return jnp.maximum(h, 0), (h >= 0) & (counts[jnp.maximum(h, 0)] > 0)

    def pair(g, half, k, h, n):
        mine = force_mine(spread, rows, g, half)
        force_pair(mine, beads, h, n, table, acc, sums[half] if k else None)

    first()
    tile_loop(tiles, width, counts, 1 + nbr.shape[1], partner, pair, tasks)
    last()


def ghost_force_kernel(
    faces,
    upper,
    cap,
    reach,
    where,
    counts,
    face_nbr,
    cross_pair,
    a_table,
    union,
    spread,
    density,
    face,
    near,
    flip,
    below,
    above,
    face_rho,
    pair_rho,
    below_rho,
    above_rho,
    own_out,
    face_out,
    pair_out,
    below_out,
    above_out,
    ghosts,
    beads,
    acc,
    rho,
    rows_0,
    rows_1,
    sums_0,
    sums_1,
    reduced,
    meta,
    meta_smem,
    sem,
):
    tiles, width = union.shape[0], union.shape[2]
    rows, sums = (rows_0, rows_1), (sums_0, sums_1)
    gather_ghosts(ghosts, face, near, flip, below, above)
    ghost_meta(ghosts, faces, upper, meta, meta_smem, sem)
    zero(acc, own_out, *sums)
    table = amplitudes(a_table)
    columns = face_nbr.shape[1] + cross_pair.shape[1]
    at = 0
    for ref in (face_rho, pair_rho, below_rho, above_rho):
        rho[pl.ds(at, ref.shape[0]), :] = ref[...]
        at += ref.shape[0]
    for t in range(ghosts.shape[0]):
        ghosts[t] = force_tile(ghosts, rho[pl.ds(t, 1), :], t)
    for t in range(tiles):
        beads[t] = force_tile(union, density[pl.ds(t, 1), :], t)

    first, tasks, last = force_tasks(tiles, beads, rows, sums, own_out)

    def partner(g, k):
        return ghost_partner(
            k, g, face_nbr, cross_pair, where, meta_smem, faces, upper, cap, reach
        )

    def pair(g, half, k, h, n):
        mine = force_mine(spread, rows, g, half)
        force_pair(mine, ghosts, h, n, table, acc, sums[half])

    first()
    tile_loop(tiles, width, counts, columns, partner, pair, tasks)
    last()
    for c in range(3):
        for t in range(acc.shape[1]):
            reduced[pl.ds(t, 1), :] = jnp.sum(acc[c, t], axis=0, keepdims=True)
        face_out[c] = reduced[pl.ds(0, faces)]
        pair_out[c] = reduced[pl.ds(faces, 2 * upper)]
        below_out[c] = reduced[pl.ds(faces + 2 * upper, 2 * upper)]
        above_out[c] = reduced[pl.ds(faces + 4 * upper, 2 * upper)]


def finish_kernel(counts, pos, vel, local_acc, ghost_acc, face_back, top_back, pos_out, vel_out):
    tiles, width = local_acc.shape[1], local_acc.shape[3]
    faces, upper = face_back.shape[1], top_back.shape[1]
    lane = lax.broadcasted_iota(jnp.int32, (1, width), 1)
    for g in range(tiles):
        cols = pl.ds(g * width, width)
        live = lane < counts[g]
        for c in range(3):
            force = jnp.sum(local_acc[c, g] + ghost_acc[c, g], axis=0, keepdims=True)
            if g < faces:
                force = force + face_back[c, pl.ds(g, 1), :]
            if g >= tiles - upper:
                force = force + top_back[c, pl.ds(g - (tiles - upper), 1), :]
            speed = jnp.where(live, vel[pl.ds(c, 1), cols] + time_step * force, 0.0)
            vel_out[pl.ds(c, 1), cols] = speed
            place = jnp.where(live, pos[pl.ds(c, 1), cols] + time_step * speed, 0.0)
            pos_out[pl.ds(c, 1), cols] = place


def on_device(
    layers,
    places,
    positions,
    velocities,
    types,
    counts,
    a_table,
    local_nbr,
    face_nbr,
    cross_send,
    cross_pair,
):
    tiles = counts.shape[0]
    width = positions.shape[1] // tiles
    faces, upper = tiles // 4, tiles // 2
    offsets, cap = cross_send.shape[1], cross_send.shape[2]
    reach = offsets // 2
    total = faces + 6 * upper
    both = ("layer", "lat")

    def lateral(value, by):
        return lax.ppermute(value, "lat", [(m, (m + by) % places) for m in range(places)])

    def swap(value):
        return lax.ppermute(value, "lat", [(m, m ^ 1) for m in range(places)])

    def climb(value, by, flip=0):
        return lax.ppermute(
            value,
            both,
            [
                (l * places + m, ((l + by) % layers) * places + (m ^ flip))
                for l in range(layers)
                for m in range(places)
            ],
        )

    kinds = types.reshape(tiles, width)
    payload, top, face = pl.pallas_call(
        pack_kernel,
        out_shape=(sds(tiles, 8, width), sds(upper, 8, width), sds(faces, 8, width)),
        in_specs=[VMEM, VMEM, VMEM, SMEM, SMEM],
        out_specs=[VMEM] * 3,
        compiler_params=params(),
    )(positions, velocities, kinds, counts, cross_send)
    near = climb(top, 1)
    flip = climb(top, 1, 1)
    face_ghosts = lateral(face, 1)
    chip_ghosts = jnp.concatenate([near, flip], axis=0)
    below = lateral(chip_ghosts, 2)
    above = lateral(chip_ghosts, -2)
    where = jnp.stack([lax.axis_index("layer"), lax.axis_index("lat") % 2]).astype(jnp.int32)

    square = pltpu.VMEM((width, width), f32)
    square_1 = pltpu.VMEM((1, width, width), f32)
    square_3 = pltpu.VMEM((3, width, width), f32)
    local_acc, spread = pl.pallas_call(
        local_density_kernel,
        out_shape=(sds(tiles, 8, width), sds(tiles, 7, width, width)),
        in_specs=[SMEM, SMEM, VMEM],
        out_specs=[VMEM] * 2,
        scratch_shapes=[square_3, square_3, square_1, square_1],
        cost_estimate=pl.CostEstimate(flops=200 * 10**6, bytes_accessed=10**6, transcendentals=0),
        compiler_params=params(),
    )(counts, local_nbr, payload)

    sizes = (faces, upper, cap, reach)
    meta_scratch = [
        pltpu.VMEM((total, width), jnp.int32),
        pltpu.SMEM((total, width), jnp.int32),
        pltpu.SemaphoreType.DMA,
    ]
    own, own_top, face_part, pair_part, below_part, above_part = pl.pallas_call(
        functools.partial(ghost_density_kernel, *sizes),
        out_shape=(
            sds(tiles, width),
            sds(upper, width),
            sds(faces, width),
            sds(2 * upper, width),
            sds(2 * upper, width),
            sds(2 * upper, width),
        ),
        in_specs=[SMEM] * 4 + [VMEM] * 7,
        out_specs=[VMEM] * 6,
        scratch_shapes=[
            pltpu.VMEM((total, 8, width), f32),
            pltpu.VMEM((total, 8, width), f32),
            pltpu.VMEM((tiles, 8, width), f32),
            square_1,
            square_1,
            pltpu.VMEM((total, width), f32),
        ]
        + meta_scratch,
        compiler_params=params(),
    )(
        where,
        counts,
        face_nbr,
        cross_pair,
        spread,
        local_acc,
        face_ghosts,
        near,
        flip,
        below,
        above,
    )

    owner_part = climb(own_top, 1)
    from_above = lateral(below_part, -2)
    from_below = lateral(above_part, 2)
    face_back = lateral(face_part, -1)
    met = pair_part + from_above + from_below
    met = jnp.concatenate([met[:upper] + owner_part, met[upper:]], axis=0)
    other = swap(met)
    pair_rho = met + jnp.concatenate([other[upper:], other[:upper]], axis=0)
    top_rho = climb(pair_rho[:upper], -1)
    below_rho = lateral(pair_rho, 2)
    above_rho = lateral(pair_rho, -2)
    bottom_rho = own[:faces] + face_back
    face_rho = lateral(bottom_rho, 1)
    density = jnp.concatenate([bottom_rho, own[faces : tiles - upper], top_rho], axis=0)

    ghost_acc, face_force, pair_force, below_force, above_force = pl.pallas_call(
        functools.partial(ghost_force_kernel, *sizes),
        out_shape=(
            sds(3, tiles, 8, width),
            sds(3, faces, width),
            sds(3, 2 * upper, width),
            sds(3, 2 * upper, width),
            sds(3, 2 * upper, width),
        ),
        in_specs=[SMEM] * 5 + [VMEM] * 12,
        out_specs=[VMEM] * 5,
        scratch_shapes=[
            pltpu.VMEM((total, 8, width), f32),
            pltpu.VMEM((tiles, 8, width), f32),
            pltpu.VMEM((3, total, 8, width), f32),
            pltpu.VMEM((total, width), f32),
            square,
            square,
            square_3,
            square_3,
            pltpu.VMEM((total, width), f32),
        ]
        + meta_scratch,
        compiler_params=params(),
    )(
        where,
        counts,
        face_nbr,
        cross_pair,
        a_table,
        payload,
        spread,
        density,
        face_ghosts,
        near,
        flip,
        below,
        above,
        face_rho,
        pair_rho,
        below_rho,
        above_rho,
    )

    force_face = lateral(face_force, -1)
    force_met = pair_force + lateral(below_force, -2) + lateral(above_force, 2)
    force_other = swap(force_met[:, upper:])
    force_top = climb(force_met[:, :upper] + force_other, -1)

    local_force = pl.pallas_call(
        local_force_kernel,
        out_shape=sds(3, tiles, 8, width),
        in_specs=[SMEM, SMEM, SMEM, VMEM, VMEM, VMEM],
        out_specs=VMEM,
        scratch_shapes=[
            pltpu.VMEM((tiles, 8, width), f32),
            square,
            square,
            square_3,
            square_3,
        ],
        cost_estimate=pl.CostEstimate(flops=400 * 10**6, bytes_accessed=10**6, transcendentals=0),
        compiler_params=params(),
    )(counts, local_nbr, a_table, payload, spread, density)

    return pl.pallas_call(
        finish_kernel,
        out_shape=(sds(*positions.shape), sds(*velocities.shape)),
        in_specs=[SMEM] + [VMEM] * 6,
        out_specs=[VMEM] * 2,
        compiler_params=params(),
    )(counts, positions, velocities, local_force, ghost_acc, force_face, force_top)


def solution(mesh):
    placed = (
        P(None, ("layer", "lat")),
        P(None, ("layer", "lat")),
        P(("layer", "lat")),
        P(("layer", "lat")),
        P(),
        P(("layer", "lat"), None),
        P(("layer", "lat"), None),
        P(("layer", "lat"), None, None),
        P(("layer", "lat"), None),
    )
    return jax.shard_map(
        functools.partial(on_device, mesh.shape["layer"], mesh.shape["lat"]),
        mesh=mesh,
        in_specs=placed,
        out_specs=(P(None, ("layer", "lat")), P(None, ("layer", "lat"))),
        check_vma=False,
    )
```

```python
import functools
import math

import jax
import jax.numpy as jnp
from jax import lax
from jax.experimental import pallas as pl
from jax.experimental.pallas import tpu as pltpu
from jax.sharding import PartitionSpec as P

cutoff_density = 0.75
density_norm = 15.0 / (2.0 * math.pi * cutoff_density**3)
repulse = 25.0
friction = 4.5
time_step = 0.01
distance_floor = 0.01
far_away = 10000.0
density_scale = density_norm / (cutoff_density * cutoff_density)
crowd_scale = repulse / cutoff_density
VMEM = pl.BlockSpec(memory_space=pltpu.VMEM)
SMEM = pl.BlockSpec(memory_space=pltpu.SMEM)
HBM = pl.BlockSpec(memory_space=pltpu.HBM)
f32 = jnp.float32


def sds(*shape):
    return jax.ShapeDtypeStruct(shape, f32)


def params():
    return pltpu.CompilerParams(vmem_limit_bytes=32 * 1024 * 1024)


def fetch(sems, *copies):
    started = [pltpu.make_async_copy(a, b, sems.at[i]) for i, (a, b) in enumerate(copies)]
    for copy in started:
        copy.start()

    def wait():
        for copy in started:
            copy.wait()

    return wait


def pack_kernel(
    pos_hbm, vel_hbm, typ_hbm, counts_hbm, send_hbm, out, top, face, pos, vel, typ, counts, send, sems
):
    fetch(
        sems, (pos_hbm, pos), (vel_hbm, vel), (typ_hbm, typ), (counts_hbm, counts), (send_hbm, send)
    )()
    tiles = out.shape[0]
    width = out.shape[2]
    lane = lax.broadcasted_iota(jnp.int32, (1, width), 1)
    upper = top.shape[0]
    offsets, cap = send.shape[0], send.shape[2]
    for g in range(tiles):
        cols = pl.ds(g * width, width)
        live = lane < counts[g]
        for c in range(3):
            out[g, pl.ds(c, 1), :] = jnp.where(live, pos[pl.ds(c, 1), cols], far_away)
            out[g, pl.ds(3 + c, 1), :] = vel[pl.ds(c, 1), cols]
        out[g, pl.ds(6, 1), :] = typ[pl.ds(g, 1), :].astype(f32)
        meta = jnp.full((1, width), counts[g], jnp.int32)
        o = g - (tiles - upper)
        if 0 <= o < offsets:
            for c in range(cap):
                meta = jnp.where(lane == c, send[o, 0, c], meta)
        out[g, pl.ds(7, 1), :] = meta.astype(f32)
    top[...] = out[pl.ds(tiles - upper, upper)]
    face[...] = out[pl.ds(0, face.shape[0])]


def diagonal(width):
    lane = lax.broadcasted_iota(jnp.int32, (8, width), 1)
    return lane - lax.broadcasted_iota(jnp.int32, (8, width), 0)


def spread_row(row, store):
    width = row.shape[1]
    diff = diagonal(width)
    row = jnp.broadcast_to(row, (8, width))
    for r in range(0, width, 8):
        one = jnp.sum(jnp.where(diff == r, row, 0.0), axis=1, keepdims=True)
        store(r, jnp.broadcast_to(one, (8, width)))


def row_sums(acc, *at):
    width = acc.shape[-1]
    diff = diagonal(width)
    out = jnp.zeros((8, width), f32)
    for r in range(0, width, 8):
        out = jnp.where(diff == r, jnp.sum(acc[*at, pl.ds(r, 8), :], axis=1, keepdims=True), out)
    return out


def by_fours(tiles, body):
    def step(i, carry):
        for t in range(4):
            body(4 * i + t)
        return carry

    lax.fori_loop(0, tiles // 4, step, 0)


def fold(ref, first, *at):
    width = ref.shape[-1]
    sub = lax.broadcasted_iota(jnp.int32, (8, width), 0)
    parts = [ref[*at, first + t] for t in range(8)]
    for step in (4, 2, 1):
        low = sub % (2 * step) < step
        parts = [
            jnp.where(low, a, b) + pltpu.roll(jnp.where(low, b, a), step, 0)
            if step == 4
            else jnp.where(low, a, b)
            + jnp.where(
                low,
                pltpu.roll(jnp.where(low, b, a), 8 - step, 0),
                pltpu.roll(jnp.where(low, b, a), step, 0),
            )
            for a, b in zip(parts[:step], parts[step:])
        ]
    return parts[0]


def branch(used, count, width, body):
    sizes = (0,) + tuple(width * e // 8 for e in (4, 6, 8))
    index = jnp.where(used, 1, 0)
    for n in sizes[1:-1]:
        index += jnp.where(used & (count > n), 1, 0)

    def pick(low, high):
        if low == high:
            body(sizes[low])
            return
        middle = (low + high) // 2

        @pl.when(index <= middle)
        def _():
            pick(low, middle)

        @pl.when(index > middle)
        def _():
            pick(middle + 1, high)

    pick(0, len(sizes) - 1)


def tile_loop(tiles, width, counts, slots, partner, pair):
    def step(g, carry):
        count = counts[g]
        listed = [partner(g, k) for k in range(slots)]
        for k, (h, used) in enumerate(listed):

            def body(n, k=k, h=h):
                if n:
                    pair(g, k, h, n)

            branch(used & (count > 0), count, width, body)
        return carry

    lax.fori_loop(0, tiles, step, 0)


def column(ref, h, c):
    return jnp.broadcast_to(ref[h, pl.ds(c, 1), :], (8, ref.shape[2]))


def density_pair(mine, union, h, n, acc_cols, acc_rows, g):
    other = [column(union, h, c) for c in range(3)]
    total = None
    for r in range(0, n, 8):
        d = [mine(c, r) - other[c] for c in range(3)]
        d2 = jnp.maximum(d[0] * d[0] + d[1] * d[1] + d[2] * d[2], distance_floor)
        w = jnp.maximum(cutoff_density - d2 * lax.rsqrt(d2), 0.0)
        w = w * w
        total = w if total is None else total + w
        if acc_rows is not None:
            acc_rows[g, pl.ds(r, 8), :] += w
    acc_cols[h] += total


def force_pair(mine, union, h, n, table, acc_cols, acc_rows, g):
    a00, a01, a11 = table
    other = [column(union, h, c) for c in range(8)]
    first = a00 + other[6] * (a01 - a00)
    slope = (a01 + other[6] * (a11 - a01)) - first
    total = [None] * 3
    for r in range(0, n, 8):
        d = [mine(c, r) - other[c] for c in range(3)]
        d2 = jnp.maximum(d[0] * d[0] + d[1] * d[1] + d[2] * d[2], distance_floor)
        inverse = lax.rsqrt(d2)
        dist = d2 * inverse
        wc = jnp.maximum(1.0 - dist, 0.0)
        wd = jnp.maximum(cutoff_density - dist, 0.0)
        dv = [mine(3 + c, r) - other[3 + c] for c in range(3)]
        approach = (d[0] * dv[0] + d[1] * dv[1] + d[2] * dv[2]) * inverse
        scalar = (first + mine(6, r) * slope) - approach * wc
        scalar = scalar * wc + (mine(7, r) + other[7]) * wd
        scalar = scalar * inverse
        for c in range(3):
            push = d[c] * scalar
            total[c] = push if total[c] is None else total[c] + push
            if acc_rows is not None:
                acc_rows[c, g, pl.ds(r, 8), :] += push
    for c in range(3):
        acc_cols[c, h] -= total[c]


def zero(*refs):
    for ref in refs:
        ref[...] = jnp.zeros_like(ref)


def spread_kernel(union, spread):
    tiles = union.shape[0]

    def fill(g):
        for c in range(spread.shape[1]):

            def store(r, value, c=c):
                spread[g, c, pl.ds(r, 8), :] = value

            row = union[g, pl.ds(c, 1), :]
            spread_row(row * friction if 3 <= c < 6 else row, store)

    by_fours(tiles, fill)


def local_partner(counts, nbr):
    def partner(g, k):
        if k == 0:
            return g, True
        h = nbr[k - 1, g]
        return jnp.maximum(h, 0), (h >= 0) & (counts[jnp.maximum(h, 0)] > 0)

    return partner


def local_density_kernel(counts_hbm, nbr_hbm, union, spread, acc, sums, counts, nbr, sems):
    wait = fetch(sems, (counts_hbm, counts), (nbr_hbm, nbr))
    tiles, width = union.shape[0], union.shape[2]
    zero(sums)
    wait()
    self_term = (cutoff_density - math.sqrt(distance_floor)) ** 2
    lane = lax.broadcasted_iota(jnp.int32, (8, width), 1)
    sub = lax.broadcasted_iota(jnp.int32, (8, width), 0)
    for g in range(tiles):
        acc[g] = jnp.where((lane < counts[g]) & (sub == 0), -self_term, 0.0)

    def pair(g, k, h, n):
        mine = lambda c, r: spread[g, c, pl.ds(r, 8), :]
        density_pair(mine, union, h, n, acc, sums if k else None, g)

    tile_loop(tiles, width, counts, 1 + nbr.shape[0], local_partner(counts, nbr), pair)


def gather_ghosts(ghosts, face, near, flip, below, above):
    at = 0
    for ref in (face, near, flip, below, above):
        ghosts[pl.ds(at, ref.shape[0])] = ref[...]
        at += ref.shape[0]


def ghost_meta(ghosts, meta, meta_smem, sem):
    total = ghosts.shape[0]
    for t in range(total):
        meta[pl.ds(t, 1), :] = ghosts[t, pl.ds(7, 1), :].astype(jnp.int32)
    copy = pltpu.make_async_copy(meta, meta_smem, sem)
    copy.start()
    return copy.wait


def ghost_partner(k, g, face_nbr, cross_pair, where, meta, faces, upper, cap, reach):
    columns = face_nbr.shape[0]
    if k < columns:
        f = face_nbr[k, g]
        h = jnp.maximum(f, 0)
        return h, (f >= 0) & (meta[h, meta.shape[1] - 1] > 0)
    s = cross_pair[k - columns, g]
    layer, core = where[0], where[1]
    slot = jnp.maximum(s, 0)
    o = slot // cap
    c = slot - o * cap
    place = core - o + 2 * reach
    hop = place // 2 - 1
    flipped = jnp.where(lax.rem(place, 2) == core, 0, 1)
    hops = jnp.where(hop == 0, 0, jnp.where(hop < 0, 1, 2))
    base = faces + (hops * 2 + flipped) * upper
    u = meta[base + o, c]
    h = base + jnp.maximum(u, 0)
    return h, (s >= 0) & (layer > 0) & (u >= 0) & (meta[h, meta.shape[1] - 1] > 0)


def ghost_density_kernel(
    faces,
    upper,
    cap,
    reach,
    where,
    counts_hbm,
    face_nbr_hbm,
    cross_pair_hbm,
    spread,
    local_acc,
    local_sums,
    face,
    near,
    flip,
    below,
    above,
    own_out,
    top_out,
    face_out,
    pair_out,
    below_out,
    above_out,
    sums,
    ghosts,
    acc,
    reduced,
    counts,
    face_nbr,
    cross_pair,
    meta,
    meta_smem,
    sems,
    sem,
):
    wait = fetch(
        sems, (counts_hbm, counts), (face_nbr_hbm, face_nbr), (cross_pair_hbm, cross_pair)
    )
    tiles, width = spread.shape[0], spread.shape[2]
    gather_ghosts(ghosts, face, near, flip, below, above)
    wait_meta = ghost_meta(ghosts, meta, meta_smem, sem)
    zero(acc)
    wait()
    wait_meta()

    def partner(g, k):
        return ghost_partner(
            k, g, face_nbr, cross_pair, where, meta_smem, faces, upper, cap, reach
        )

    def pair(g, k, h, n):
        mine = lambda c, r: spread[g, c, pl.ds(r, 8), :]
        density_pair(mine, ghosts, h, n, acc, sums, g)

    slots = face_nbr.shape[0] + cross_pair.shape[0]
    tile_loop(tiles, width, counts, slots, partner, pair)
    for t in range(0, acc.shape[0], 8):
        reduced[pl.ds(t, 8), :] = fold(acc, t)
    face_out[...] = reduced[pl.ds(0, faces)]
    pair_out[...] = reduced[pl.ds(faces, 2 * upper)]
    below_out[...] = reduced[pl.ds(faces + 2 * upper, 2 * upper)]
    above_out[...] = reduced[pl.ds(faces + 4 * upper, 2 * upper)]

    def collect(t):
        acc[t] = local_acc[t] + row_sums(sums, t)

    by_fours(tiles, collect)
    for t in range(0, tiles, 8):
        own_out[pl.ds(t, 8), :] = fold(acc, t)
    top_out[...] = own_out[pl.ds(tiles - upper, upper)]


def force_tile(union, density, t):
    tile = union[t]
    channel = lax.broadcasted_iota(jnp.int32, tile.shape, 0)
    tile = jnp.where((channel >= 3) & (channel < 6), tile * friction, tile)
    return jnp.where(channel == 7, density * (crowd_scale * density_scale), tile)


def amplitudes(a_table):
    return (a_table[0, 0], 0.5 * (a_table[0, 1] + a_table[1, 0]), a_table[1, 1])


def force_mine(spread, crowd, g):
    def mine(c, r):
        return crowd[g, pl.ds(r, 8), :] if c == 7 else spread[g, c, pl.ds(r, 8), :]

    return mine


def local_force_kernel(
    counts_hbm,
    nbr_hbm,
    a_table,
    union,
    spread,
    crowd,
    density,
    acc,
    beads,
    sums,
    counts,
    nbr,
    sems,
):
    wait = fetch(sems, (counts_hbm, counts), (nbr_hbm, nbr))
    tiles, width = union.shape[0], union.shape[2]
    table = amplitudes(a_table)
    zero(acc, sums)
    for t in range(tiles):
        beads[t] = force_tile(union, density[pl.ds(t, 1), :], t)
    wait()

    def pair(g, k, h, n):
        force_pair(force_mine(spread, crowd, g), beads, h, n, table, acc, sums if k else None, g)

    tile_loop(tiles, width, counts, 1 + nbr.shape[0], local_partner(counts, nbr), pair)

    def collect(t):
        for c in range(3):
            acc[c, t] += row_sums(sums, c, t)

    by_fours(tiles, collect)


def ghost_force_kernel(
    faces,
    upper,
    cap,
    reach,
    where,
    counts_hbm,
    face_nbr_hbm,
    cross_pair_hbm,
    a_table,
    union,
    spread,
    density,
    face,
    near,
    flip,
    below,
    above,
    face_rho,
    pair_rho,
    below_rho,
    above_rho,
    own_out,
    crowd,
    face_out,
    pair_out,
    below_out,
    above_out,
    ghosts,
    acc,
    rho,
    sums,
    reduced,
    counts,
    face_nbr,
    cross_pair,
    meta,
    meta_smem,
    sems,
    sem,
):
    wait = fetch(
        sems, (counts_hbm, counts), (face_nbr_hbm, face_nbr), (cross_pair_hbm, cross_pair)
    )
    tiles, width = union.shape[0], union.shape[2]
    gather_ghosts(ghosts, face, near, flip, below, above)
    wait_meta = ghost_meta(ghosts, meta, meta_smem, sem)
    zero(acc, sums)
    table = amplitudes(a_table)
    at = 0
    for ref in (face_rho, pair_rho, below_rho, above_rho):
        rho[pl.ds(at, ref.shape[0]), :] = ref[...]
        at += ref.shape[0]
    for t in range(ghosts.shape[0]):
        ghosts[t] = force_tile(ghosts, rho[pl.ds(t, 1), :], t)

    def fill(g):
        def store(r, value):
            crowd[g, pl.ds(r, 8), :] = value

        spread_row(density[pl.ds(g, 1), :] * (crowd_scale * density_scale), store)

    by_fours(tiles, fill)
    wait()
    wait_meta()

    def partner(g, k):
        return ghost_partner(
            k, g, face_nbr, cross_pair, where, meta_smem, faces, upper, cap, reach
        )

    def pair(g, k, h, n):
        force_pair(force_mine(spread, crowd, g), ghosts, h, n, table, acc, sums, g)

    slots = face_nbr.shape[0] + cross_pair.shape[0]
    tile_loop(tiles, width, counts, slots, partner, pair)
    for c in range(3):
        for t in range(0, acc.shape[1], 8):
            reduced[pl.ds(t, 8), :] = fold(acc, t, c)
        face_out[c] = reduced[pl.ds(0, faces)]
        pair_out[c] = reduced[pl.ds(faces, 2 * upper)]
        below_out[c] = reduced[pl.ds(faces + 2 * upper, 2 * upper)]
        above_out[c] = reduced[pl.ds(faces + 4 * upper, 2 * upper)]

    def collect(t):
        for c in range(3):
            own_out[c, t] = row_sums(sums, c, t)

    by_fours(tiles, collect)


def finish_kernel(counts, pos, vel, local_acc, ghost_acc, face_back, top_back, pos_out, vel_out, force):
    tiles, width = local_acc.shape[1], local_acc.shape[3]
    faces, upper = face_back.shape[1], top_back.shape[1]
    lane = lax.broadcasted_iota(jnp.int32, (1, width), 1)

    def add(t):
        for c in range(3):
            force[c, t] = local_acc[c, t] + ghost_acc[c, t]

    for t in range(tiles):
        add(t)
    for c in range(3):
        for t in range(0, tiles, 8):
            total = fold(force, t, c)
            if t < faces:
                total = total + face_back[c, pl.ds(t, 8), :]
            if t >= tiles - upper:
                total = total + top_back[c, pl.ds(t - (tiles - upper), 8), :]
            for i in range(8):
                g = t + i
                cols = pl.ds(g * width, width)
                live = lane < counts[g]
                speed = vel[pl.ds(c, 1), cols] + time_step * total[i : i + 1]
                speed = jnp.where(live, speed, 0.0)
                vel_out[pl.ds(c, 1), cols] = speed
                place = jnp.where(live, pos[pl.ds(c, 1), cols] + time_step * speed, 0.0)
                pos_out[pl.ds(c, 1), cols] = place


def on_device(
    layers,
    places,
    positions,
    velocities,
    types,
    counts,
    a_table,
    local_nbr,
    face_nbr,
    cross_send,
    cross_pair,
):
    tiles = counts.shape[0]
    width = positions.shape[1] // tiles
    faces, upper = tiles // 4, tiles // 2
    offsets, cap = cross_send.shape[1], cross_send.shape[2]
    reach = offsets // 2
    total = faces + 6 * upper
    both = ("layer", "lat")

    def lateral(value, by):
        return lax.ppermute(value, "lat", [(m, (m + by) % places) for m in range(places)])

    def swap(value):
        return lax.ppermute(value, "lat", [(m, m ^ 1) for m in range(places)])

    def climb(value, by, flip=0):
        return lax.ppermute(
            value,
            both,
            [
                (l * places + m, ((l + by) % layers) * places + (m ^ flip))
                for l in range(layers)
                for m in range(places)
            ],
        )

    kinds = types.reshape(tiles, width)
    local_nbr, face_nbr, cross_pair = local_nbr.T, face_nbr.T, cross_pair.T
    send = cross_send.transpose(1, 0, 2)
    ints = jnp.int32
    counts_smem = pltpu.SMEM((tiles,), ints)
    payload, top, face = pl.pallas_call(
        pack_kernel,
        out_shape=(sds(tiles, 8, width), sds(upper, 8, width), sds(faces, 8, width)),
        in_specs=[HBM] * 5,
        out_specs=[VMEM] * 3,
        scratch_shapes=[
            pltpu.VMEM(positions.shape, f32),
            pltpu.VMEM(velocities.shape, f32),
            pltpu.VMEM(kinds.shape, ints),
            counts_smem,
            pltpu.SMEM(send.shape, ints),
            pltpu.SemaphoreType.DMA((5,)),
        ],
        compiler_params=params(),
    )(positions, velocities, kinds, counts, send)
    spread = pl.pallas_call(
        spread_kernel,
        out_shape=sds(tiles, 7, width, width),
        in_specs=[VMEM],
        out_specs=VMEM,
        cost_estimate=pl.CostEstimate(flops=10**9, bytes_accessed=15 * 10**6, transcendentals=0),
        compiler_params=params(),
    )(payload)
    near = climb(top, 1)
    flip = climb(top, 1, 1)
    face_ghosts = lateral(face, 1)
    chip_ghosts = jnp.concatenate([near, flip], axis=0)
    below = lateral(chip_ghosts, 2)
    above = lateral(chip_ghosts, -2)
    where = jnp.stack([lax.axis_index("layer"), lax.axis_index("lat") % 2]).astype(jnp.int32)

    local_acc, local_sums = pl.pallas_call(
        local_density_kernel,
        out_shape=(sds(tiles, 8, width), sds(tiles, width, width)),
        in_specs=[HBM, HBM, VMEM, VMEM],
        out_specs=[VMEM] * 2,
        scratch_shapes=[
            counts_smem,
            pltpu.SMEM(local_nbr.shape, ints),
            pltpu.SemaphoreType.DMA((2,)),
        ],
        cost_estimate=pl.CostEstimate(flops=10**9, bytes_accessed=15 * 10**6, transcendentals=0),
        compiler_params=params(),
    )(counts, local_nbr, payload, spread)

    sizes = (faces, upper, cap, reach)
    tables = [
        counts_smem,
        pltpu.SMEM(face_nbr.shape, ints),
        pltpu.SMEM(cross_pair.shape, ints),
        pltpu.VMEM((total, width), ints),
        pltpu.SMEM((total, width), ints),
        pltpu.SemaphoreType.DMA((3,)),
        pltpu.SemaphoreType.DMA,
    ]
    own, own_top, face_part, pair_part, below_part, above_part, _ = pl.pallas_call(
        functools.partial(ghost_density_kernel, *sizes),
        out_shape=(
            sds(tiles, width),
            sds(upper, width),
            sds(faces, width),
            sds(2 * upper, width),
            sds(2 * upper, width),
            sds(2 * upper, width),
            sds(tiles, width, width),
        ),
        in_specs=[SMEM] + [HBM] * 3 + [VMEM] * 8,
        out_specs=[VMEM] * 7,
        scratch_shapes=[
            pltpu.VMEM((total, 8, width), f32),
            pltpu.VMEM((total, 8, width), f32),
            pltpu.VMEM((total, width), f32),
        ]
        + tables,
        input_output_aliases={6: 6},
        compiler_params=params(),
    )(
        where,
        counts,
        face_nbr,
        cross_pair,
        spread,
        local_acc,
        local_sums,
        face_ghosts,
        near,
        flip,
        below,
        above,
    )

    owner_part = climb(own_top, 1)
    from_above = lateral(below_part, -2)
    from_below = lateral(above_part, 2)
    face_back = lateral(face_part, -1)
    met = pair_part + from_above + from_below
    met = jnp.concatenate([met[:upper] + owner_part, met[upper:]], axis=0)
    other = swap(met)
    pair_rho = met + jnp.concatenate([other[upper:], other[:upper]], axis=0)
    top_rho = climb(pair_rho[:upper], -1)
    below_rho = lateral(pair_rho, 2)
    above_rho = lateral(pair_rho, -2)
    bottom_rho = own[:faces] + face_back
    face_rho = lateral(bottom_rho, 1)
    density = jnp.concatenate([bottom_rho, own[faces : tiles - upper], top_rho], axis=0)

    ghost_acc, crowd, face_force, pair_force, below_force, above_force = pl.pallas_call(
        functools.partial(ghost_force_kernel, *sizes),
        out_shape=(
            sds(3, tiles, 8, width),
            sds(tiles, width, width),
            sds(3, faces, width),
            sds(3, 2 * upper, width),
            sds(3, 2 * upper, width),
            sds(3, 2 * upper, width),
        ),
        in_specs=[SMEM] + [HBM] * 3 + [SMEM] + [VMEM] * 12,
        out_specs=[VMEM] * 6,
        scratch_shapes=[
            pltpu.VMEM((total, 8, width), f32),
            pltpu.VMEM((3, total, 8, width), f32),
            pltpu.VMEM((total, width), f32),
            pltpu.VMEM((3, tiles, width, width), f32),
            pltpu.VMEM((total, width), f32),
        ]
        + tables,
        compiler_params=params(),
    )(
        where,
        counts,
        face_nbr,
        cross_pair,
        a_table,
        payload,
        spread,
        density,
        face_ghosts,
        near,
        flip,
        below,
        above,
        face_rho,
        pair_rho,
        below_rho,
        above_rho,
    )

    force_face = lateral(face_force, -1)
    force_met = pair_force + lateral(below_force, -2) + lateral(above_force, 2)
    force_other = swap(force_met[:, upper:])
    force_top = climb(force_met[:, :upper] + force_other, -1)

    local_force = pl.pallas_call(
        local_force_kernel,
        out_shape=sds(3, tiles, 8, width),
        in_specs=[HBM, HBM, SMEM] + [VMEM] * 4,
        out_specs=VMEM,
        scratch_shapes=[
            pltpu.VMEM((tiles, 8, width), f32),
            pltpu.VMEM((3, tiles, width, width), f32),
            counts_smem,
            pltpu.SMEM(local_nbr.shape, ints),
            pltpu.SemaphoreType.DMA((2,)),
        ],
        cost_estimate=pl.CostEstimate(flops=2 * 10**9, bytes_accessed=20 * 10**6, transcendentals=0),
        compiler_params=params(),
    )(counts, local_nbr, a_table, payload, spread, crowd, density)

    return pl.pallas_call(
        finish_kernel,
        out_shape=(sds(*positions.shape), sds(*velocities.shape)),
        in_specs=[SMEM] + [VMEM] * 6,
        out_specs=[VMEM] * 2,
        scratch_shapes=[pltpu.VMEM((3, tiles, 8, width), f32)],
        compiler_params=params(),
    )(counts, positions, velocities, local_force, ghost_acc, force_face, force_top)


def solution(mesh):
    placed = (
        P(None, ("layer", "lat")),
        P(None, ("layer", "lat")),
        P(("layer", "lat")),
        P(("layer", "lat")),
        P(),
        P(("layer", "lat"), None),
        P(("layer", "lat"), None),
        P(("layer", "lat"), None, None),
        P(("layer", "lat"), None),
    )
    return jax.shard_map(
        functools.partial(on_device, mesh.shape["layer"], mesh.shape["lat"]),
        mesh=mesh,
        in_specs=placed,
        out_specs=(P(None, ("layer", "lat")), P(None, ("layer", "lat"))),
        check_vma=False,
    )
```

```python
import functools
import math

import jax
import jax.numpy as jnp
from jax import lax
from jax.experimental import pallas as pl
from jax.experimental.pallas import tpu as pltpu
from jax.sharding import PartitionSpec as P

cutoff_density = 0.75
density_norm = 15.0 / (2.0 * math.pi * cutoff_density**3)
repulse = 25.0
friction = 4.5
time_step = 0.01
distance_floor = 0.01
far_away = 10000.0
density_scale = density_norm / (cutoff_density * cutoff_density)
crowd_scale = repulse / cutoff_density
VMEM = pl.BlockSpec(memory_space=pltpu.VMEM)
SMEM = pl.BlockSpec(memory_space=pltpu.SMEM)
HBM = pl.BlockSpec(memory_space=pltpu.HBM)
f32 = jnp.float32


def sds(*shape):
    return jax.ShapeDtypeStruct(shape, f32)


def params(mib=24):
    return pltpu.CompilerParams(vmem_limit_bytes=mib * 1024 * 1024)


def in_hbm(value):
    return pltpu.with_memory_space_constraint(value, pltpu.HBM)


def fetch(sems, *copies):
    started = [pltpu.make_async_copy(a, b, sems.at[i]) for i, (a, b) in enumerate(copies)]
    for copy in started:
        copy.start()

    def wait():
        for copy in started:
            copy.wait()

    return wait


def pack_kernel(
    pos_hbm, vel_hbm, typ_hbm, counts_hbm, send_hbm, out, top, face, pos, vel, typ, counts, send, sems
):
    fetch(
        sems, (pos_hbm, pos), (vel_hbm, vel), (typ_hbm, typ), (counts_hbm, counts), (send_hbm, send)
    )()
    tiles = out.shape[0]
    width = out.shape[2]
    lane = lax.broadcasted_iota(jnp.int32, (1, width), 1)
    upper = top.shape[0]
    offsets, cap = send.shape[0], send.shape[2]
    for g in range(tiles):
        cols = pl.ds(g * width, width)
        live = lane < counts[g]
        for c in range(3):
            out[g, pl.ds(c, 1), :] = jnp.where(live, pos[pl.ds(c, 1), cols], far_away)
            out[g, pl.ds(3 + c, 1), :] = vel[pl.ds(c, 1), cols]
        out[g, pl.ds(6, 1), :] = typ[pl.ds(g, 1), :].astype(f32)
        meta = jnp.full((1, width), counts[g], jnp.int32)
        o = g - (tiles - upper)
        if 0 <= o < offsets:
            for c in range(cap):
                meta = jnp.where(lane == c, send[o, 0, c], meta)
        out[g, pl.ds(7, 1), :] = meta.astype(f32)
    top[...] = out[pl.ds(tiles - upper, upper)]
    face[...] = out[pl.ds(0, face.shape[0])]


def diagonal(width):
    lane = lax.broadcasted_iota(jnp.int32, (8, width), 1)
    return lane - lax.broadcasted_iota(jnp.int32, (8, width), 0)


def spread_row(row, store):
    width = row.shape[1]
    diff = diagonal(width)
    row = jnp.broadcast_to(row, (8, width))
    for r in range(0, width, 8):
        one = jnp.sum(jnp.where(diff == r, row, 0.0), axis=1, keepdims=True)
        store(r, jnp.broadcast_to(one, (8, width)))


def row_sums(acc, *at):
    width = acc.shape[-1]
    diff = diagonal(width)
    out = jnp.zeros((8, width), f32)
    for r in range(0, width, 8):
        out = jnp.where(diff == r, jnp.sum(acc[*at, pl.ds(r, 8), :], axis=1, keepdims=True), out)
    return out


def by_fours(tiles, body):
    def step(i, carry):
        for t in range(4):
            body(4 * i + t)
        return carry

    lax.fori_loop(0, tiles // 4, step, 0)


def fold(ref, first, *at):
    width = ref.shape[-1]
    sub = lax.broadcasted_iota(jnp.int32, (8, width), 0)
    parts = [ref[*at, first + t] for t in range(8)]
    for step in (4, 2, 1):
        low = sub % (2 * step) < step
        parts = [
            jnp.where(low, a, b) + pltpu.roll(jnp.where(low, b, a), step, 0)
            if step == 4
            else jnp.where(low, a, b)
            + jnp.where(
                low,
                pltpu.roll(jnp.where(low, b, a), 8 - step, 0),
                pltpu.roll(jnp.where(low, b, a), step, 0),
            )
            for a, b in zip(parts[:step], parts[step:])
        ]
    return parts[0]


def branch(used, count, width, body):
    sizes = (0,) + tuple(width * e // 8 for e in (4, 6, 8))
    index = jnp.where(used, 1, 0)
    for n in sizes[1:-1]:
        index += jnp.where(used & (count > n), 1, 0)

    def pick(low, high):
        if low == high:
            body(sizes[low])
            return
        middle = (low + high) // 2

        @pl.when(index <= middle)
        def _():
            pick(low, middle)

        @pl.when(index > middle)
        def _():
            pick(middle + 1, high)

    pick(0, len(sizes) - 1)


def tile_loop(tiles, width, counts, slots, partner, pair):
    def step(g, carry):
        count = counts[g]
        listed = [partner(g, k) for k in range(slots)]
        for k, (h, used) in enumerate(listed):

            def body(n, k=k, h=h):
                if n:
                    pair(g, k, h, n)

            branch(used & (count > 0), count, width, body)
        return carry

    lax.fori_loop(0, tiles, step, 0)


def column(ref, h, c):
    return jnp.broadcast_to(ref[h, pl.ds(c, 1), :], (8, ref.shape[2]))


def density_pair(mine, union, h, n, acc_cols, acc_rows, g):
    other = [column(union, h, c) for c in range(3)]
    total = None
    for r in range(0, n, 8):
        d = [mine(c, r) - other[c] for c in range(3)]
        d2 = jnp.maximum(d[0] * d[0] + d[1] * d[1] + d[2] * d[2], distance_floor)
        w = jnp.maximum(cutoff_density - d2 * lax.rsqrt(d2), 0.0)
        w = w * w
        total = w if total is None else total + w
        if acc_rows is not None:
            acc_rows[g, pl.ds(r, 8), :] += w
    acc_cols[h] += total


def force_pair(mine, union, h, n, table, acc_cols, acc_rows, g):
    a00, a01, a11 = table
    other = [column(union, h, c) for c in range(8)]
    first = a00 + other[6] * (a01 - a00)
    slope = (a01 + other[6] * (a11 - a01)) - first
    total = [None] * 3
    for r in range(0, n, 8):
        d = [mine(c, r) - other[c] for c in range(3)]
        d2 = jnp.maximum(d[0] * d[0] + d[1] * d[1] + d[2] * d[2], distance_floor)
        inverse = lax.rsqrt(d2)
        dist = d2 * inverse
        wc = jnp.maximum(1.0 - dist, 0.0)
        wd = jnp.maximum(cutoff_density - dist, 0.0)
        dv = [mine(3 + c, r) - other[3 + c] for c in range(3)]
        approach = (d[0] * dv[0] + d[1] * dv[1] + d[2] * dv[2]) * inverse
        scalar = (first + mine(6, r) * slope) - approach * wc
        scalar = scalar * wc + (mine(7, r) + other[7]) * wd
        scalar = scalar * inverse
        for c in range(3):
            push = d[c] * scalar
            total[c] = push if total[c] is None else total[c] + push
            if acc_rows is not None:
                acc_rows[c, g, pl.ds(r, 8), :] += push
    for c in range(3):
        acc_cols[c, h] -= total[c]


def zero(*refs):
    for ref in refs:
        ref[...] = jnp.zeros_like(ref)


def spread_kernel(union, spread):
    tiles = union.shape[0]

    def fill(g):
        for c in range(spread.shape[1]):

            def store(r, value, c=c):
                spread[g, c, pl.ds(r, 8), :] = value

            row = union[g, pl.ds(c, 1), :]
            spread_row(row * friction if 3 <= c < 6 else row, store)

    by_fours(tiles, fill)


def local_partner(counts, nbr):
    def partner(g, k):
        if k == 0:
            return g, True
        h = nbr[k - 1, g]
        return jnp.maximum(h, 0), (h >= 0) & (counts[jnp.maximum(h, 0)] > 0)

    return partner


def local_density_kernel(counts_hbm, nbr_hbm, union, spread, acc, sums, counts, nbr, sems):
    wait = fetch(sems, (counts_hbm, counts), (nbr_hbm, nbr))
    tiles, width = union.shape[0], union.shape[2]
    zero(sums)
    wait()
    self_term = (cutoff_density - math.sqrt(distance_floor)) ** 2
    lane = lax.broadcasted_iota(jnp.int32, (8, width), 1)
    sub = lax.broadcasted_iota(jnp.int32, (8, width), 0)
    for g in range(tiles):
        acc[g] = jnp.where((lane < counts[g]) & (sub == 0), -self_term, 0.0)

    def pair(g, k, h, n):
        mine = lambda c, r: spread[g, c, pl.ds(r, 8), :]
        density_pair(mine, union, h, n, acc, sums if k else None, g)

    tile_loop(tiles, width, counts, 1 + nbr.shape[0], local_partner(counts, nbr), pair)


def gather(target, *refs):
    at = 0
    for ref in refs:
        target[pl.ds(at, ref.shape[0])] = ref[...]
        at += ref.shape[0]


def spill(target, at, *refs):
    for ref in refs:
        ref[...] = target[pl.ds(at, ref.shape[0])]
        at += ref.shape[0]


def ghost_meta(ghosts, meta, meta_smem, sem):
    total = ghosts.shape[0]
    for t in range(total):
        meta[pl.ds(t, 1), :] = ghosts[t, pl.ds(7, 1), :].astype(jnp.int32)
    copy = pltpu.make_async_copy(meta, meta_smem, sem)
    copy.start()
    return copy.wait


def ghost_partner(k, g, face_nbr, cross_pair, where, meta, faces, upper, cap, reach):
    columns = face_nbr.shape[0]
    if k < columns:
        f = face_nbr[k, g]
        h = jnp.maximum(f, 0)
        return h, (f >= 0) & (meta[h, meta.shape[1] - 1] > 0)
    s = cross_pair[k - columns, g]
    layer, core = where[0], where[1]
    slot = jnp.maximum(s, 0)
    o = slot // cap
    c = slot - o * cap
    place = core - o + 2 * reach
    hop = place // 2 - 1
    flipped = jnp.where(lax.rem(place, 2) == core, 0, 1)
    hops = jnp.where(hop == 0, 0, jnp.where(hop < 0, 1, 2))
    base = faces + (hops * 2 + flipped) * upper
    u = meta[base + o, c]
    h = base + jnp.maximum(u, 0)
    return h, (s >= 0) & (layer > 0) & (u >= 0) & (meta[h, meta.shape[1] - 1] > 0)


def ghost_density_kernel(
    faces,
    upper,
    cap,
    reach,
    where,
    counts_hbm,
    face_nbr_hbm,
    cross_pair_hbm,
    spread,
    local_acc,
    local_sums,
    face,
    near,
    flip,
    below,
    above,
    own_out,
    top_out,
    face_out,
    pair_out,
    below_out,
    above_out,
    sums,
    listed,
    ghosts,
    acc,
    reduced,
    counts,
    face_nbr,
    cross_pair,
    meta,
    meta_smem,
    sems,
    sem,
):
    wait = fetch(
        sems, (counts_hbm, counts), (face_nbr_hbm, face_nbr), (cross_pair_hbm, cross_pair)
    )
    tiles, width = spread.shape[0], spread.shape[2]
    gather(ghosts, face, near, flip, below, above)
    wait_meta = ghost_meta(ghosts, meta, meta_smem, sem)
    wait()
    wait_meta()
    zero(acc)
    slots = face_nbr.shape[0] + cross_pair.shape[0]
    for g in range(tiles):
        for k in range(slots):
            h, ok = ghost_partner(
                k, g, face_nbr, cross_pair, where, meta_smem, faces, upper, cap, reach
            )
            listed[k, g] = jnp.where(ok & (counts[g] > 0), h, -1)

    def partner(g, k):
        h = listed[k, g]
        return jnp.maximum(h, 0), h >= 0

    def pair(g, k, h, n):
        mine = lambda c, r: spread[g, c, pl.ds(r, 8), :]
        density_pair(mine, ghosts, h, n, acc, sums, g)

    tile_loop(tiles, width, counts, slots, partner, pair)
    for t in range(0, acc.shape[0], 8):
        reduced[pl.ds(t, 8), :] = fold(acc, t)
    face_out[...] = reduced[pl.ds(0, faces)]
    spill(reduced, faces, pair_out)
    below_out[pl.ds(0, 2 * upper)] = reduced[pl.ds(faces + 2 * upper, 2 * upper)]
    below_out[pl.ds(2 * upper, faces)] = reduced[pl.ds(0, faces)]
    spill(reduced, faces + 4 * upper, above_out)

    def collect(t):
        acc[t] = local_acc[t] + row_sums(sums, t)

    by_fours(tiles, collect)
    for t in range(0, tiles, 8):
        own_out[pl.ds(t, 8), :] = fold(acc, t)
    top_out[...] = own_out[pl.ds(tiles - upper, upper)]


def force_tile(union, density, t):
    tile = union[t]
    channel = lax.broadcasted_iota(jnp.int32, tile.shape, 0)
    tile = jnp.where((channel >= 3) & (channel < 6), tile * friction, tile)
    return jnp.where(channel == 7, density * (crowd_scale * density_scale), tile)


def amplitudes(a_table):
    return (a_table[0, 0], 0.5 * (a_table[0, 1] + a_table[1, 0]), a_table[1, 1])


def force_mine(spread, crowd, g):
    def mine(c, r):
        return crowd[g, pl.ds(r, 8), :] if c == 7 else spread[g, c, pl.ds(r, 8), :]

    return mine


def listed_partner(listed, first, shift):
    def partner(g, k):
        h = listed[first + k, g]
        return jnp.maximum(h - shift, 0), h >= 0

    return partner


def cross_force_kernel(
    columns,
    faces,
    counts_hbm,
    listed_hbm,
    a_table,
    spread,
    density,
    near,
    flip,
    below,
    above,
    pair_rho,
    below_rho,
    above_rho,
    crowd,
    own_out,
    pair_out,
    below_out,
    above_out,
    sums,
    ghosts,
    acc,
    rho,
    reduced,
    counts,
    listed,
    sems,
):
    wait = fetch(sems, (counts_hbm, counts), (listed_hbm, listed))
    tiles, width = spread.shape[0], spread.shape[2]
    zero(acc, sums)
    table = amplitudes(a_table)
    gather(ghosts, near, flip, below, above)
    gather(rho, pair_rho, below_rho, above_rho)
    for t in range(ghosts.shape[0]):
        ghosts[t] = force_tile(ghosts, rho[pl.ds(t, 1), :], t)

    def fill(g):
        def store(r, value):
            crowd[g, pl.ds(r, 8), :] = value

        spread_row(density[pl.ds(g, 1), :] * (crowd_scale * density_scale), store)

    by_fours(tiles, fill)
    wait()

    def pair(g, k, h, n):
        force_pair(force_mine(spread, crowd, g), ghosts, h, n, table, acc, sums, g)

    partner = listed_partner(listed, columns, faces)
    tile_loop(tiles, width, counts, listed.shape[0] - columns, partner, pair)
    for c in range(3):
        for t in range(0, acc.shape[1], 8):
            reduced[pl.ds(t, 8), :] = fold(acc, t, c)
        spill(reduced, 0, pair_out.at[c], below_out.at[c], above_out.at[c])

    def collect(t):
        for c in range(3):
            own_out[c, t] = row_sums(sums, c, t)

    by_fours(tiles, collect)


def face_force_kernel(
    columns,
    counts_hbm,
    listed_hbm,
    a_table,
    spread,
    crowd,
    cross_acc,
    face,
    face_rho,
    own_out,
    face_out,
    sums,
    ghosts,
    acc,
    counts,
    listed,
    sems,
):
    wait = fetch(sems, (counts_hbm, counts), (listed_hbm, listed))
    tiles, width = spread.shape[0], spread.shape[2]
    zero(acc, sums)
    table = amplitudes(a_table)
    for t in range(ghosts.shape[0]):
        ghosts[t] = force_tile(face, face_rho[pl.ds(t, 1), :], t)
    wait()

    def pair(g, k, h, n):
        force_pair(force_mine(spread, crowd, g), ghosts, h, n, table, acc, sums, g)

    tile_loop(tiles, width, counts, columns, listed_partner(listed, 0, 0), pair)
    for c in range(3):
        for t in range(0, acc.shape[1], 8):
            face_out[c, pl.ds(t, 8), :] = fold(acc, t, c)

    def collect(t):
        for c in range(3):
            own_out[c, t] = cross_acc[c, t] + row_sums(sums, c, t)

    by_fours(tiles, collect)


def local_force_kernel(
    counts_hbm,
    nbr_hbm,
    a_table,
    union,
    spread,
    crowd,
    density,
    ghost_acc,
    acc,
    beads,
    sums,
    counts,
    nbr,
    sems,
):
    wait = fetch(sems, (counts_hbm, counts), (nbr_hbm, nbr))
    tiles, width = union.shape[0], union.shape[2]
    table = amplitudes(a_table)
    acc[...] = ghost_acc[...]
    zero(sums)
    for t in range(tiles):
        beads[t] = force_tile(union, density[pl.ds(t, 1), :], t)
    wait()

    def pair(g, k, h, n):
        force_pair(force_mine(spread, crowd, g), beads, h, n, table, acc, sums if k else None, g)

    tile_loop(tiles, width, counts, 1 + nbr.shape[0], local_partner(counts, nbr), pair)

    def collect(t):
        for c in range(3):
            acc[c, t] += row_sums(sums, c, t)

    by_fours(tiles, collect)


def finish_kernel(counts, pos, vel, acc, face_back, top_back, pos_out, vel_out):
    tiles, width = acc.shape[1], acc.shape[3]
    faces, upper = face_back.shape[1], top_back.shape[1]
    lane = lax.broadcasted_iota(jnp.int32, (1, width), 1)
    for c in range(3):
        for t in range(0, tiles, 8):
            total = fold(acc, t, c)
            if t < faces:
                total = total + face_back[c, pl.ds(t, 8), :]
            if t >= tiles - upper:
                total = total + top_back[c, pl.ds(t - (tiles - upper), 8), :]
            for i in range(8):
                g = t + i
                cols = pl.ds(g * width, width)
                live = lane < counts[g]
                speed = vel[pl.ds(c, 1), cols] + time_step * total[i : i + 1]
                speed = jnp.where(live, speed, 0.0)
                vel_out[pl.ds(c, 1), cols] = speed
                place = jnp.where(live, pos[pl.ds(c, 1), cols] + time_step * speed, 0.0)
                pos_out[pl.ds(c, 1), cols] = place


def on_device(
    layers,
    places,
    positions,
    velocities,
    types,
    counts,
    a_table,
    local_nbr,
    face_nbr,
    cross_send,
    cross_pair,
):
    tiles = counts.shape[0]
    width = positions.shape[1] // tiles
    faces, upper = tiles // 4, tiles // 2
    offsets, cap = cross_send.shape[1], cross_send.shape[2]
    reach = offsets // 2
    total = faces + 6 * upper
    both = ("layer", "lat")

    def lateral(value, by):
        return lax.ppermute(value, "lat", [(m, (m + by) % places) for m in range(places)])

    def swap(value):
        return lax.ppermute(value, "lat", [(m, m ^ 1) for m in range(places)])

    def climb(value, by, flip=0):
        return lax.ppermute(
            value,
            both,
            [
                (l * places + m, ((l + by) % layers) * places + (m ^ flip))
                for l in range(layers)
                for m in range(places)
            ],
        )

    kinds = types.reshape(tiles, width)
    local_nbr, face_nbr, cross_pair = (
        in_hbm(table.T) for table in (local_nbr, face_nbr, cross_pair)
    )
    send = in_hbm(cross_send.transpose(1, 0, 2))
    counts_hbm = in_hbm(counts)
    ints = jnp.int32
    counts_smem = pltpu.SMEM((tiles,), ints)
    payload, top, face = pl.pallas_call(
        pack_kernel,
        out_shape=(sds(tiles, 8, width), sds(upper, 8, width), sds(faces, 8, width)),
        in_specs=[HBM] * 5,
        out_specs=[VMEM] * 3,
        scratch_shapes=[
            pltpu.VMEM(positions.shape, f32),
            pltpu.VMEM(velocities.shape, f32),
            pltpu.VMEM(kinds.shape, ints),
            counts_smem,
            pltpu.SMEM(send.shape, ints),
            pltpu.SemaphoreType.DMA((5,)),
        ],
        compiler_params=params(),
    )(in_hbm(positions), in_hbm(velocities), in_hbm(kinds), counts_hbm, send)
    near = climb(top, 1)
    flip = climb(top, 1, 1)
    face_ghosts = lateral(face, 1)
    spread = pl.pallas_call(
        spread_kernel,
        out_shape=sds(tiles, 7, width, width),
        in_specs=[VMEM],
        out_specs=VMEM,
        cost_estimate=pl.CostEstimate(flops=10**9, bytes_accessed=15 * 10**6, transcendentals=0),
        compiler_params=params(),
    )(payload)
    near, flip, spread = lax.optimization_barrier((near, flip, spread))
    chip_ghosts = jnp.concatenate([near, flip], axis=0)
    below = lateral(chip_ghosts, 2)
    above = lateral(chip_ghosts, -2)
    where = jnp.stack([lax.axis_index("layer"), lax.axis_index("lat") % 2]).astype(jnp.int32)

    local_acc, local_sums = pl.pallas_call(
        local_density_kernel,
        out_shape=(sds(tiles, 8, width), sds(tiles, width, width)),
        in_specs=[HBM, HBM, VMEM, VMEM],
        out_specs=[VMEM] * 2,
        scratch_shapes=[
            counts_smem,
            pltpu.SMEM(local_nbr.shape, ints),
            pltpu.SemaphoreType.DMA((2,)),
        ],
        cost_estimate=pl.CostEstimate(flops=10**9, bytes_accessed=15 * 10**6, transcendentals=0),
        compiler_params=params(),
    )(counts_hbm, local_nbr, payload, spread)

    sizes = (faces, upper, cap, reach)
    tables = [
        counts_smem,
        pltpu.SMEM(face_nbr.shape, ints),
        pltpu.SMEM(cross_pair.shape, ints),
        pltpu.VMEM((total, width), ints),
        pltpu.SMEM((total, width), ints),
        pltpu.SemaphoreType.DMA((3,)),
        pltpu.SemaphoreType.DMA,
    ]
    own, own_top, face_part, pair_part, below_part, above_part, _, listed = pl.pallas_call(
        functools.partial(ghost_density_kernel, *sizes),
        out_shape=(
            sds(tiles, width),
            sds(upper, width),
            sds(faces, width),
            sds(2 * upper, width),
            sds(2 * upper + faces, width),
            sds(2 * upper, width),
            sds(tiles, width, width),
            jax.ShapeDtypeStruct((face_nbr.shape[0] + cross_pair.shape[0], tiles), ints),
        ),
        in_specs=[SMEM] + [HBM] * 3 + [VMEM] * 8,
        out_specs=[VMEM] * 7 + [SMEM],
        scratch_shapes=[
            pltpu.VMEM((total, 8, width), f32),
            pltpu.VMEM((total, 8, width), f32),
            pltpu.VMEM((total, width), f32),
        ]
        + tables,
        input_output_aliases={6: 6},
        compiler_params=params(),
    )(
        where,
        counts_hbm,
        face_nbr,
        cross_pair,
        spread,
        local_acc,
        local_sums,
        face_ghosts,
        near,
        flip,
        below,
        above,
    )

    pairs = 2 * upper
    odd = where[1] == 1
    owner_part = climb(own_top, 1)
    from_above = lateral(below_part, -2)
    from_below = lateral(above_part, 2)
    passed = jnp.where(odd, face_part, from_above[pairs:])
    met = pair_part + from_above[:pairs] + from_below
    met = jnp.concatenate([met[:upper] + owner_part, met[upper:]], axis=0)
    other = swap(jnp.concatenate([met, passed, own[:faces]], axis=0))
    pair_rho = met + jnp.concatenate([other[upper:pairs], other[:upper]], axis=0)
    bottom_rho = own[:faces] + other[pairs : pairs + faces]
    other_rho = passed + other[pairs + faces :]
    top_rho = climb(pair_rho[:upper], -1)
    below_rho = lateral(jnp.concatenate([pair_rho, other_rho], axis=0), 2)
    above_rho = lateral(pair_rho, -2)
    face_rho = jnp.where(odd, other_rho, below_rho[pairs:])
    below_rho = below_rho[:pairs]
    density = jnp.concatenate([bottom_rho, own[faces : tiles - upper], top_rho], axis=0)

    listed = in_hbm(listed)
    columns = face_nbr.shape[0]
    small = [
        counts_smem,
        pltpu.SMEM(listed.shape, ints),
        pltpu.SemaphoreType.DMA((2,)),
    ]
    crowd, cross_acc, pair_force, below_force, above_force = pl.pallas_call(
        functools.partial(cross_force_kernel, columns, faces),
        out_shape=(
            sds(tiles, width, width),
            sds(3, tiles, 8, width),
            sds(3, pairs, width),
            sds(3, pairs, width),
            sds(3, pairs, width),
        ),
        in_specs=[HBM] * 2 + [SMEM] + [VMEM] * 9,
        out_specs=[VMEM] * 5,
        scratch_shapes=[
            pltpu.VMEM((3, tiles, width, width), f32),
            pltpu.VMEM((3 * pairs, 8, width), f32),
            pltpu.VMEM((3, 3 * pairs, 8, width), f32),
            pltpu.VMEM((3 * pairs, width), f32),
            pltpu.VMEM((3 * pairs, width), f32),
        ]
        + small,
        compiler_params=params(),
    )(
        counts_hbm,
        listed,
        a_table,
        spread,
        density,
        near,
        flip,
        below,
        above,
        pair_rho,
        below_rho,
        above_rho,
    )
    from_above = lateral(below_force, -2)
    from_below = lateral(above_force, 2)
    ghost_acc, face_force = pl.pallas_call(
        functools.partial(face_force_kernel, columns),
        out_shape=(sds(3, tiles, 8, width), sds(3, faces, width)),
        in_specs=[HBM] * 2 + [SMEM] + [VMEM] * 5,
        out_specs=[VMEM] * 2,
        scratch_shapes=[
            pltpu.VMEM((3, tiles, width, width), f32),
            pltpu.VMEM((faces, 8, width), f32),
            pltpu.VMEM((3, faces, 8, width), f32),
        ]
        + small,
        cost_estimate=pl.CostEstimate(flops=10**9, bytes_accessed=20 * 10**6, transcendentals=0),
        compiler_params=params(),
    )(counts_hbm, listed, a_table, spread, crowd, cross_acc, face_ghosts, face_rho)
    from_above, from_below, face_force = lax.optimization_barrier(
        (from_above, from_below, face_force)
    )
    force_face = lateral(face_force, -1)
    force_met = pair_force + from_above + from_below
    force_other = swap(force_met[:, upper:])
    force_top = climb(force_met[:, :upper] + force_other, -1)

    force = pl.pallas_call(
        local_force_kernel,
        out_shape=sds(3, tiles, 8, width),
        in_specs=[HBM, HBM, SMEM] + [VMEM] * 5,
        out_specs=VMEM,
        scratch_shapes=[
            pltpu.VMEM((tiles, 8, width), f32),
            pltpu.VMEM((3, tiles, width, width), f32),
            counts_smem,
            pltpu.SMEM(local_nbr.shape, ints),
            pltpu.SemaphoreType.DMA((2,)),
        ],
        cost_estimate=pl.CostEstimate(flops=2 * 10**9, bytes_accessed=20 * 10**6, transcendentals=0),
        compiler_params=params(),
    )(counts_hbm, local_nbr, a_table, payload, spread, crowd, density, ghost_acc)

    return pl.pallas_call(
        finish_kernel,
        out_shape=(sds(*positions.shape), sds(*velocities.shape)),
        in_specs=[SMEM] + [VMEM] * 5,
        out_specs=[VMEM] * 2,
        compiler_params=params(),
    )(counts, positions, velocities, force, force_face, force_top)


def solution(mesh):
    placed = (
        P(None, ("layer", "lat")),
        P(None, ("layer", "lat")),
        P(("layer", "lat")),
        P(("layer", "lat")),
        P(),
        P(("layer", "lat"), None),
        P(("layer", "lat"), None),
        P(("layer", "lat"), None, None),
        P(("layer", "lat"), None),
    )
    return jax.shard_map(
        functools.partial(on_device, mesh.shape["layer"], mesh.shape["lat"]),
        mesh=mesh,
        in_specs=placed,
        out_specs=(P(None, ("layer", "lat")), P(None, ("layer", "lat"))),
        check_vma=False,
    )
```

```python
import functools
import math

import jax
import jax.numpy as jnp
from jax import lax
from jax.experimental import pallas as pl
from jax.experimental.pallas import tpu as pltpu
from jax.sharding import PartitionSpec as P

cutoff_density = 0.75
density_norm = 15.0 / (2.0 * math.pi * cutoff_density**3)
repulse = 25.0
friction = 4.5
time_step = 0.01
distance_floor = 0.01
far_away = 10000.0
SIZES = (4, 5, 6, 7, 8)
density_scale = density_norm / (cutoff_density * cutoff_density)
crowd_scale = repulse / cutoff_density
VMEM = pl.BlockSpec(memory_space=pltpu.VMEM)
SMEM = pl.BlockSpec(memory_space=pltpu.SMEM)
HBM = pl.BlockSpec(memory_space=pltpu.HBM)
f32 = jnp.float32


def sds(*shape):
    return jax.ShapeDtypeStruct(shape, f32)


def params(mib=16):
    return pltpu.CompilerParams(vmem_limit_bytes=mib * 1024 * 1024)


def in_hbm(value):
    return pltpu.with_memory_space_constraint(value, pltpu.HBM)


def fetch(sems, *copies):
    started = [pltpu.make_async_copy(a, b, sems.at[i]) for i, (a, b) in enumerate(copies)]
    for copy in started:
        copy.start()

    def wait():
        for copy in started:
            copy.wait()

    return wait


def pack_kernel(
    pos_hbm, vel_hbm, typ_hbm, counts_hbm, send_hbm, out, top, face, pos, vel, typ, counts, send, sems
):
    fetch(
        sems, (pos_hbm, pos), (vel_hbm, vel), (typ_hbm, typ), (counts_hbm, counts), (send_hbm, send)
    )()
    tiles = out.shape[0]
    width = out.shape[2]
    lane = lax.broadcasted_iota(jnp.int32, (1, width), 1)
    upper = top.shape[0]
    offsets, cap = send.shape[0], send.shape[2]
    for g in range(tiles):
        cols = pl.ds(g * width, width)
        live = lane < counts[g]
        for c in range(3):
            out[g, pl.ds(c, 1), :] = jnp.where(live, pos[pl.ds(c, 1), cols], far_away)
            out[g, pl.ds(3 + c, 1), :] = vel[pl.ds(c, 1), cols]
        out[g, pl.ds(6, 1), :] = typ[pl.ds(g, 1), :].astype(f32)
        meta = jnp.full((1, width), counts[g], jnp.int32)
        o = g - (tiles - upper)
        if 0 <= o < offsets:
            for c in range(cap):
                meta = jnp.where(lane == c, send[o, 0, c], meta)
        out[g, pl.ds(7, 1), :] = meta.astype(f32)
    top[...] = out[pl.ds(tiles - upper, upper)]
    face[...] = out[pl.ds(0, face.shape[0])]


def diagonal(width):
    lane = lax.broadcasted_iota(jnp.int32, (8, width), 1)
    return lane - lax.broadcasted_iota(jnp.int32, (8, width), 0)


def spread_row(row, store):
    width = row.shape[1]
    diff = diagonal(width)
    row = jnp.broadcast_to(row, (8, width))
    for r in range(0, width, 8):
        one = jnp.sum(jnp.where(diff == r, row, 0.0), axis=1, keepdims=True)
        store(r, jnp.broadcast_to(one, (8, width)))


def row_sums(acc, *at):
    width = acc.shape[-1]
    diff = diagonal(width)
    out = jnp.zeros((8, width), f32)
    for r in range(0, width, 8):
        out = jnp.where(diff == r, jnp.sum(acc[*at, pl.ds(r, 8), :], axis=1, keepdims=True), out)
    return out


def by_fours(tiles, body):
    def step(i, carry):
        for t in range(4):
            body(4 * i + t)
        return carry

    lax.fori_loop(0, tiles // 4, step, 0)


def fold(ref, first, *at):
    width = ref.shape[-1]
    sub = lax.broadcasted_iota(jnp.int32, (8, width), 0)
    parts = [ref[*at, first + t] for t in range(8)]
    for step in (4, 2, 1):
        low = sub % (2 * step) < step
        parts = [
            jnp.where(low, a, b) + pltpu.roll(jnp.where(low, b, a), step, 0)
            if step == 4
            else jnp.where(low, a, b)
            + jnp.where(
                low,
                pltpu.roll(jnp.where(low, b, a), 8 - step, 0),
                pltpu.roll(jnp.where(low, b, a), step, 0),
            )
            for a, b in zip(parts[:step], parts[step:])
        ]
    return parts[0]


def branch(used, count, width, body):
    sizes = (0,) + tuple(width * e // 8 for e in SIZES)
    index = jnp.where(used, 1, 0)
    for n in sizes[1:-1]:
        index += jnp.where(used & (count > n), 1, 0)

    def pick(low, high):
        if low == high:
            body(sizes[low])
            return
        middle = (low + high) // 2

        @pl.when(index <= middle)
        def _():
            pick(low, middle)

        @pl.when(index > middle)
        def _():
            pick(middle + 1, high)

    pick(0, len(sizes) - 1)


def tile_loop(tiles, width, counts, slots, partner, pair):
    def step(g, carry):
        count = counts[g]
        listed = [partner(g, k) for k in range(slots)]
        for k, (h, used) in enumerate(listed):

            def body(n, k=k, h=h):
                if n:
                    pair(g, k, h, n)

            branch(used & (count > 0), count, width, body)
        return carry

    lax.fori_loop(0, tiles, step, 0)


def column(ref, h, c):
    return jnp.broadcast_to(ref[h, pl.ds(c, 1), :], (8, ref.shape[2]))


def density_pair(mine, union, h, n, acc_cols, acc_rows, g):
    other = [column(union, h, c) for c in range(3)]
    total = None
    for r in range(0, n, 8):
        d = [mine(c, r) - other[c] for c in range(3)]
        d2 = jnp.maximum(d[0] * d[0] + d[1] * d[1] + d[2] * d[2], distance_floor)
        w = jnp.maximum(cutoff_density - d2 * lax.rsqrt(d2), 0.0)
        w = w * w
        total = w if total is None else total + w
        if acc_rows is not None:
            acc_rows[g, pl.ds(r, 8), :] += w
    acc_cols[h] += total


def force_pair(mine, union, h, n, table, acc_cols, acc_rows, g):
    a00, a01, a11 = table
    other = [column(union, h, c) for c in range(8)]
    first = a00 + other[6] * (a01 - a00)
    slope = (a01 + other[6] * (a11 - a01)) - first
    total = [None] * 3
    for r in range(0, n, 8):
        d = [mine(c, r) - other[c] for c in range(3)]
        d2 = jnp.maximum(d[0] * d[0] + d[1] * d[1] + d[2] * d[2], distance_floor)
        inverse = lax.rsqrt(d2)
        dist = d2 * inverse
        wc = jnp.maximum(1.0 - dist, 0.0)
        wd = jnp.maximum(cutoff_density - dist, 0.0)
        dv = [mine(3 + c, r) - other[3 + c] for c in range(3)]
        approach = (d[0] * dv[0] + d[1] * dv[1] + d[2] * dv[2]) * inverse
        scalar = (first + mine(6, r) * slope) - approach * wc
        scalar = scalar * wc + (mine(7, r) + other[7]) * wd
        scalar = scalar * inverse
        for c in range(3):
            push = d[c] * scalar
            total[c] = push if total[c] is None else total[c] + push
            if acc_rows is not None:
                acc_rows[c, g, pl.ds(r, 8), :] += push
    for c in range(3):
        acc_cols[c, h] -= total[c]


def zero(*refs):
    for ref in refs:
        ref[...] = jnp.zeros_like(ref)


def spread_kernel(union, spread):
    tiles = union.shape[0]

    def fill(g):
        for c in range(spread.shape[1]):

            def store(r, value, c=c):
                spread[g, c, pl.ds(r, 8), :] = value

            row = union[g, pl.ds(c, 1), :]
            spread_row(row * friction if 3 <= c < 6 else row, store)

    by_fours(tiles, fill)


def local_partner(counts, nbr):
    def partner(g, k):
        if k == 0:
            return g, True
        h = nbr[k - 1, g]
        return jnp.maximum(h, 0), (h >= 0) & (counts[jnp.maximum(h, 0)] > 0)

    return partner


def local_density_kernel(counts_hbm, nbr_hbm, union, spread, acc, sums, counts, nbr, sems):
    wait = fetch(sems, (counts_hbm, counts), (nbr_hbm, nbr))
    tiles, width = union.shape[0], union.shape[2]
    zero(sums)
    wait()
    self_term = (cutoff_density - math.sqrt(distance_floor)) ** 2
    lane = lax.broadcasted_iota(jnp.int32, (8, width), 1)
    sub = lax.broadcasted_iota(jnp.int32, (8, width), 0)
    for g in range(tiles):
        acc[g] = jnp.where((lane < counts[g]) & (sub == 0), -self_term, 0.0)

    def pair(g, k, h, n):
        mine = lambda c, r: spread[g, c, pl.ds(r, 8), :]
        density_pair(mine, union, h, n, acc, sums if k else None, g)

    tile_loop(tiles, width, counts, 1 + nbr.shape[0], local_partner(counts, nbr), pair)


def gather(target, *refs):
    at = 0
    for ref in refs:
        target[pl.ds(at, ref.shape[0])] = ref[...]
        at += ref.shape[0]


def spill(target, at, *refs):
    for ref in refs:
        ref[...] = target[pl.ds(at, ref.shape[0])]
        at += ref.shape[0]


def ghost_meta(ghosts, meta, meta_smem, sem):
    total = ghosts.shape[0]
    for t in range(total):
        meta[pl.ds(t, 1), :] = ghosts[t, pl.ds(7, 1), :].astype(jnp.int32)
    copy = pltpu.make_async_copy(meta, meta_smem, sem)
    copy.start()
    return copy.wait


def ghost_partner(k, g, face_nbr, cross_pair, where, meta, faces, upper, cap, reach):
    columns = face_nbr.shape[0]
    if k < columns:
        f = face_nbr[k, g]
        h = jnp.maximum(f, 0)
        return h, (f >= 0) & (meta[h, meta.shape[1] - 1] > 0)
    s = cross_pair[k - columns, g]
    layer, core = where[0], where[1]
    slot = jnp.maximum(s, 0)
    o = slot // cap
    c = slot - o * cap
    place = core - o + 2 * reach
    hop = place // 2 - 1
    flipped = jnp.where(lax.rem(place, 2) == core, 0, 1)
    hops = jnp.where(hop == 0, 0, jnp.where(hop < 0, 1, 2))
    base = faces + (hops * 2 + flipped) * upper
    u = meta[base + o, c]
    h = base + jnp.maximum(u, 0)
    return h, (s >= 0) & (layer > 0) & (u >= 0) & (meta[h, meta.shape[1] - 1] > 0)


def ghost_density_kernel(
    faces,
    upper,
    cap,
    reach,
    where,
    counts_hbm,
    face_nbr_hbm,
    cross_pair_hbm,
    spread,
    local_acc,
    local_sums,
    face,
    near,
    flip,
    below,
    above,
    own_out,
    top_out,
    face_out,
    pair_out,
    below_out,
    above_out,
    sums,
    listed,
    ghosts,
    acc,
    reduced,
    counts,
    face_nbr,
    cross_pair,
    meta,
    meta_smem,
    sems,
    sem,
):
    wait = fetch(
        sems, (counts_hbm, counts), (face_nbr_hbm, face_nbr), (cross_pair_hbm, cross_pair)
    )
    tiles, width = spread.shape[0], spread.shape[2]
    gather(ghosts, face, near, flip, below, above)
    wait_meta = ghost_meta(ghosts, meta, meta_smem, sem)
    wait()
    wait_meta()
    zero(acc)
    slots = face_nbr.shape[0] + cross_pair.shape[0]
    for g in range(tiles):
        for k in range(slots):
            h, ok = ghost_partner(
                k, g, face_nbr, cross_pair, where, meta_smem, faces, upper, cap, reach
            )
            listed[k, g] = jnp.where(ok & (counts[g] > 0), h, -1)

    def partner(g, k):
        h = listed[k, g]
        return jnp.maximum(h, 0), h >= 0

    def pair(g, k, h, n):
        mine = lambda c, r: spread[g, c, pl.ds(r, 8), :]
        density_pair(mine, ghosts, h, n, acc, sums, g)

    tile_loop(tiles, width, counts, slots, partner, pair)
    for t in range(0, acc.shape[0], 8):
        reduced[pl.ds(t, 8), :] = fold(acc, t)
    face_out[...] = reduced[pl.ds(0, faces)]
    spill(reduced, faces, pair_out)
    below_out[pl.ds(0, 2 * upper)] = reduced[pl.ds(faces + 2 * upper, 2 * upper)]
    below_out[pl.ds(2 * upper, faces)] = reduced[pl.ds(0, faces)]
    spill(reduced, faces + 4 * upper, above_out)

    def collect(t):
        acc[t] = local_acc[t] + row_sums(sums, t)

    by_fours(tiles, collect)
    for t in range(0, tiles, 8):
        own_out[pl.ds(t, 8), :] = fold(acc, t)
    top_out[...] = own_out[pl.ds(tiles - upper, upper)]


def force_tile(union, density, t):
    tile = union[t]
    channel = lax.broadcasted_iota(jnp.int32, tile.shape, 0)
    tile = jnp.where((channel >= 3) & (channel < 6), tile * friction, tile)
    return jnp.where(channel == 7, density * (crowd_scale * density_scale), tile)


def amplitudes(a_table):
    return (a_table[0, 0], 0.5 * (a_table[0, 1] + a_table[1, 0]), a_table[1, 1])


def force_mine(spread, crowd, g):
    def mine(c, r):
        return crowd[g, pl.ds(r, 8), :] if c == 7 else spread[g, c, pl.ds(r, 8), :]

    return mine


def listed_partner(listed, first, shift):
    def partner(g, k):
        h = listed[first + k, g]
        return jnp.maximum(h - shift, 0), h >= 0

    return partner


def cross_force_kernel(
    columns,
    faces,
    counts_hbm,
    listed_hbm,
    a_table,
    spread,
    density,
    near,
    flip,
    below,
    above,
    pair_rho,
    below_rho,
    above_rho,
    crowd,
    sums,
    pair_out,
    below_out,
    above_out,
    ghosts,
    acc,
    rho,
    reduced,
    counts,
    listed,
    sems,
):
    wait = fetch(sems, (counts_hbm, counts), (listed_hbm, listed))
    tiles, width = spread.shape[0], spread.shape[2]
    zero(acc, sums)
    table = amplitudes(a_table)
    gather(ghosts, near, flip, below, above)
    gather(rho, pair_rho, below_rho, above_rho)
    for t in range(ghosts.shape[0]):
        ghosts[t] = force_tile(ghosts, rho[pl.ds(t, 1), :], t)

    def fill(g):
        def store(r, value):
            crowd[g, pl.ds(r, 8), :] = value

        spread_row(density[pl.ds(g, 1), :] * (crowd_scale * density_scale), store)

    by_fours(tiles, fill)
    wait()

    def pair(g, k, h, n):
        force_pair(force_mine(spread, crowd, g), ghosts, h, n, table, acc, sums, g)

    partner = listed_partner(listed, columns, faces)
    tile_loop(tiles, width, counts, listed.shape[0] - columns, partner, pair)
    for c in range(3):
        for t in range(0, acc.shape[1], 8):
            reduced[pl.ds(t, 8), :] = fold(acc, t, c)
        spill(reduced, 0, pair_out.at[c], below_out.at[c], above_out.at[c])


def face_force_kernel(
    columns,
    counts_hbm,
    listed_hbm,
    a_table,
    spread,
    crowd,
    cross_sums,
    face,
    face_rho,
    sums,
    face_out,
    ghosts,
    acc,
    counts,
    listed,
    sems,
):
    wait = fetch(sems, (counts_hbm, counts), (listed_hbm, listed))
    tiles, width = spread.shape[0], spread.shape[2]
    zero(acc)
    sums[...] = cross_sums[...]
    table = amplitudes(a_table)
    for t in range(ghosts.shape[0]):
        ghosts[t] = force_tile(face, face_rho[pl.ds(t, 1), :], t)
    wait()

    def pair(g, k, h, n):
        force_pair(force_mine(spread, crowd, g), ghosts, h, n, table, acc, sums, g)

    tile_loop(tiles, width, counts, columns, listed_partner(listed, 0, 0), pair)
    for c in range(3):
        for t in range(0, acc.shape[1], 8):
            face_out[c, pl.ds(t, 8), :] = fold(acc, t, c)


def local_force_kernel(
    counts_hbm,
    nbr_hbm,
    a_table,
    union,
    spread,
    crowd,
    density,
    ghost_sums,
    acc,
    beads,
    sums,
    counts,
    nbr,
    sems,
):
    wait = fetch(sems, (counts_hbm, counts), (nbr_hbm, nbr))
    tiles, width = union.shape[0], union.shape[2]
    table = amplitudes(a_table)
    zero(acc)
    sums[...] = ghost_sums[...]
    for t in range(tiles):
        beads[t] = force_tile(union, density[pl.ds(t, 1), :], t)
    wait()

    def pair(g, k, h, n):
        force_pair(force_mine(spread, crowd, g), beads, h, n, table, acc, sums if k else None, g)

    tile_loop(tiles, width, counts, 1 + nbr.shape[0], local_partner(counts, nbr), pair)

    def collect(t):
        for c in range(3):
            acc[c, t] += row_sums(sums, c, t)

    by_fours(tiles, collect)


def finish_kernel(counts, pos, vel, acc, face_back, top_back, pos_out, vel_out):
    tiles, width = acc.shape[1], acc.shape[3]
    faces, upper = face_back.shape[1], top_back.shape[1]
    lane = lax.broadcasted_iota(jnp.int32, (1, width), 1)
    for c in range(3):
        for t in range(0, tiles, 8):
            total = fold(acc, t, c)
            if t < faces:
                total = total + face_back[c, pl.ds(t, 8), :]
            if t >= tiles - upper:
                total = total + top_back[c, pl.ds(t - (tiles - upper), 8), :]
            for i in range(8):
                g = t + i
                cols = pl.ds(g * width, width)
                live = lane < counts[g]
                speed = vel[pl.ds(c, 1), cols] + time_step * total[i : i + 1]
                speed = jnp.where(live, speed, 0.0)
                vel_out[pl.ds(c, 1), cols] = speed
                place = jnp.where(live, pos[pl.ds(c, 1), cols] + time_step * speed, 0.0)
                pos_out[pl.ds(c, 1), cols] = place


def on_device(
    layers,
    places,
    positions,
    velocities,
    types,
    counts,
    a_table,
    local_nbr,
    face_nbr,
    cross_send,
    cross_pair,
):
    tiles = counts.shape[0]
    width = positions.shape[1] // tiles
    faces, upper = tiles // 4, tiles // 2
    offsets, cap = cross_send.shape[1], cross_send.shape[2]
    reach = offsets // 2
    total = faces + 6 * upper
    both = ("layer", "lat")

    def lateral(value, by):
        return lax.ppermute(value, "lat", [(m, (m + by) % places) for m in range(places)])

    def swap(value):
        return lax.ppermute(value, "lat", [(m, m ^ 1) for m in range(places)])

    def climb(value, by, flip=0):
        return lax.ppermute(
            value,
            both,
            [
                (l * places + m, ((l + by) % layers) * places + (m ^ flip))
                for l in range(layers)
                for m in range(places)
            ],
        )

    kinds = types.reshape(tiles, width)
    local_nbr, face_nbr, cross_pair = (
        in_hbm(table.T) for table in (local_nbr, face_nbr, cross_pair)
    )
    send = in_hbm(cross_send.transpose(1, 0, 2))
    counts_hbm = in_hbm(counts)
    ints = jnp.int32
    counts_smem = pltpu.SMEM((tiles,), ints)
    payload, top, face = pl.pallas_call(
        pack_kernel,
        out_shape=(sds(tiles, 8, width), sds(upper, 8, width), sds(faces, 8, width)),
        in_specs=[HBM] * 5,
        out_specs=[VMEM] * 3,
        scratch_shapes=[
            pltpu.VMEM(positions.shape, f32),
            pltpu.VMEM(velocities.shape, f32),
            pltpu.VMEM(kinds.shape, ints),
            counts_smem,
            pltpu.SMEM(send.shape, ints),
            pltpu.SemaphoreType.DMA((5,)),
        ],
        compiler_params=params(),
    )(in_hbm(positions), in_hbm(velocities), in_hbm(kinds), counts_hbm, send)
    near = climb(top, 1)
    flip = climb(top, 1, 1)
    face_ghosts = lateral(face, 1)
    def spread_rows(payload, channels):
        return pl.pallas_call(
            spread_kernel,
            out_shape=sds(tiles, channels, width, width),
            in_specs=[VMEM],
            out_specs=VMEM,
            cost_estimate=pl.CostEstimate(
                flops=10**9, bytes_accessed=15 * 10**6, transcendentals=0
            ),
            compiler_params=params(),
        )(payload)

    near = climb(top, 1)
    flip = climb(top, 1, 1)
    face_ghosts = lateral(face, 1)
    spread = spread_rows(payload, 3)
    near, flip, spread = lax.optimization_barrier((near, flip, spread))
    chip_ghosts = jnp.concatenate([near, flip], axis=0)
    below = lateral(chip_ghosts, 2)
    above = lateral(chip_ghosts, -2)
    where = jnp.stack([lax.axis_index("layer"), lax.axis_index("lat") % 2]).astype(jnp.int32)

    local_acc, local_sums = pl.pallas_call(
        local_density_kernel,
        out_shape=(sds(tiles, 8, width), sds(tiles, width, width)),
        in_specs=[HBM, HBM, VMEM, VMEM],
        out_specs=[VMEM] * 2,
        scratch_shapes=[
            counts_smem,
            pltpu.SMEM(local_nbr.shape, ints),
            pltpu.SemaphoreType.DMA((2,)),
        ],
        cost_estimate=pl.CostEstimate(flops=10**9, bytes_accessed=15 * 10**6, transcendentals=0),
        compiler_params=params(),
    )(counts_hbm, local_nbr, payload, spread)

    sizes = (faces, upper, cap, reach)
    tables = [
        counts_smem,
        pltpu.SMEM(face_nbr.shape, ints),
        pltpu.SMEM(cross_pair.shape, ints),
        pltpu.VMEM((total, width), ints),
        pltpu.SMEM((total, width), ints),
        pltpu.SemaphoreType.DMA((3,)),
        pltpu.SemaphoreType.DMA,
    ]
    own, own_top, face_part, pair_part, below_part, above_part, _, listed = pl.pallas_call(
        functools.partial(ghost_density_kernel, *sizes),
        out_shape=(
            sds(tiles, width),
            sds(upper, width),
            sds(faces, width),
            sds(2 * upper, width),
            sds(2 * upper + faces, width),
            sds(2 * upper, width),
            sds(tiles, width, width),
            jax.ShapeDtypeStruct((face_nbr.shape[0] + cross_pair.shape[0], tiles), ints),
        ),
        in_specs=[SMEM] + [HBM] * 3 + [VMEM] * 8,
        out_specs=[VMEM] * 7 + [SMEM],
        scratch_shapes=[
            pltpu.VMEM((total, 8, width), f32),
            pltpu.VMEM((total, 8, width), f32),
            pltpu.VMEM((total, width), f32),
        ]
        + tables,
        input_output_aliases={6: 6},
        compiler_params=params(),
    )(
        where,
        counts_hbm,
        face_nbr,
        cross_pair,
        spread,
        local_acc,
        local_sums,
        face_ghosts,
        near,
        flip,
        below,
        above,
    )

    pairs = 2 * upper
    odd = where[1] == 1
    owner_part = climb(own_top, 1)
    from_above = lateral(below_part, -2)
    from_below = lateral(above_part, 2)
    payload, _ = lax.optimization_barrier((payload, pair_part))
    spread = spread_rows(payload, 7)
    from_above, from_below, spread = lax.optimization_barrier((from_above, from_below, spread))
    passed = jnp.where(odd, face_part, from_above[pairs:])
    met = pair_part + from_above[:pairs] + from_below
    met = jnp.concatenate([met[:upper] + owner_part, met[upper:]], axis=0)
    other = swap(jnp.concatenate([met, passed, own[:faces]], axis=0))
    pair_rho = met + jnp.concatenate([other[upper:pairs], other[:upper]], axis=0)
    bottom_rho = own[:faces] + other[pairs : pairs + faces]
    other_rho = passed + other[pairs + faces :]
    top_rho = climb(pair_rho[:upper], -1)
    below_rho = lateral(jnp.concatenate([pair_rho, other_rho], axis=0), 2)
    above_rho = lateral(pair_rho, -2)
    face_rho = jnp.where(odd, other_rho, below_rho[pairs:])
    below_rho = below_rho[:pairs]
    density = jnp.concatenate([bottom_rho, own[faces : tiles - upper], top_rho], axis=0)

    columns = face_nbr.shape[0]
    small = [
        counts_smem,
        pltpu.SMEM(listed.shape, ints),
        pltpu.SemaphoreType.DMA((2,)),
    ]
    crowd, cross_sums, pair_force, below_force, above_force = pl.pallas_call(
        functools.partial(cross_force_kernel, columns, faces),
        out_shape=(
            sds(tiles, width, width),
            sds(3, tiles, width, width),
            sds(3, pairs, width),
            sds(3, pairs, width),
            sds(3, pairs, width),
        ),
        in_specs=[HBM] * 2 + [SMEM] + [VMEM] * 9,
        out_specs=[VMEM] * 5,
        scratch_shapes=[
            pltpu.VMEM((3 * pairs, 8, width), f32),
            pltpu.VMEM((3, 3 * pairs, 8, width), f32),
            pltpu.VMEM((3 * pairs, width), f32),
            pltpu.VMEM((3 * pairs, width), f32),
        ]
        + small,
        compiler_params=params(),
    )(
        counts_hbm,
        listed,
        a_table,
        spread,
        density,
        near,
        flip,
        below,
        above,
        pair_rho,
        below_rho,
        above_rho,
    )
    from_above = lateral(below_force, -2)
    from_below = lateral(above_force, 2)
    ghost_sums, face_force = pl.pallas_call(
        functools.partial(face_force_kernel, columns),
        out_shape=(sds(3, tiles, width, width), sds(3, faces, width)),
        in_specs=[HBM] * 2 + [SMEM] + [VMEM] * 5,
        out_specs=[VMEM] * 2,
        scratch_shapes=[
            pltpu.VMEM((faces, 8, width), f32),
            pltpu.VMEM((3, faces, 8, width), f32),
        ]
        + small,
        cost_estimate=pl.CostEstimate(flops=10**9, bytes_accessed=20 * 10**6, transcendentals=0),
        compiler_params=params(),
    )(counts_hbm, listed, a_table, spread, crowd, cross_sums, face_ghosts, face_rho)
    from_above, from_below, face_force = lax.optimization_barrier(
        (from_above, from_below, face_force)
    )
    force_face = lateral(face_force, -1)
    force_met = pair_force + from_above + from_below
    force_other = swap(force_met[:, upper:])
    force_top = climb(force_met[:, :upper] + force_other, -1)

    force = pl.pallas_call(
        local_force_kernel,
        out_shape=sds(3, tiles, 8, width),
        in_specs=[HBM, HBM, SMEM] + [VMEM] * 5,
        out_specs=VMEM,
        scratch_shapes=[
            pltpu.VMEM((tiles, 8, width), f32),
            pltpu.VMEM((3, tiles, width, width), f32),
            counts_smem,
            pltpu.SMEM(local_nbr.shape, ints),
            pltpu.SemaphoreType.DMA((2,)),
        ],
        cost_estimate=pl.CostEstimate(flops=2 * 10**9, bytes_accessed=20 * 10**6, transcendentals=0),
        compiler_params=params(),
    )(counts_hbm, local_nbr, a_table, payload, spread, crowd, density, ghost_sums)

    return pl.pallas_call(
        finish_kernel,
        out_shape=(sds(*positions.shape), sds(*velocities.shape)),
        in_specs=[SMEM] + [VMEM] * 5,
        out_specs=[VMEM] * 2,
        compiler_params=params(),
    )(counts, positions, velocities, force, force_face, force_top)


def solution(mesh):
    placed = (
        P(None, ("layer", "lat")),
        P(None, ("layer", "lat")),
        P(("layer", "lat")),
        P(("layer", "lat")),
        P(),
        P(("layer", "lat"), None),
        P(("layer", "lat"), None),
        P(("layer", "lat"), None, None),
        P(("layer", "lat"), None),
    )
    return jax.shard_map(
        functools.partial(on_device, mesh.shape["layer"], mesh.shape["lat"]),
        mesh=mesh,
        in_specs=placed,
        out_specs=(P(None, ("layer", "lat")), P(None, ("layer", "lat"))),
        check_vma=False,
    )
```

```python
import functools
import math

import jax
import jax.numpy as jnp
from jax import lax
from jax.experimental import pallas as pl
from jax.experimental.pallas import tpu as pltpu
from jax.sharding import PartitionSpec as P

cutoff_density = 0.75
density_norm = 15.0 / (2.0 * math.pi * cutoff_density**3)
repulse = 25.0
friction = 4.5
time_step = 0.01
distance_floor = 0.01
far_away = 10000.0
DENSITY_SIZES = (8,)
FORCE_SIZES = (5, 8)
density_scale = density_norm / (cutoff_density * cutoff_density)
crowd_scale = repulse / cutoff_density
VMEM = pl.BlockSpec(memory_space=pltpu.VMEM)
SMEM = pl.BlockSpec(memory_space=pltpu.SMEM)
HBM = pl.BlockSpec(memory_space=pltpu.HBM)
f32 = jnp.float32


def sds(*shape):
    return jax.ShapeDtypeStruct(shape, f32)


def params(mib=16):
    return pltpu.CompilerParams(vmem_limit_bytes=mib * 1024 * 1024)


def in_hbm(value):
    return pltpu.with_memory_space_constraint(value, pltpu.HBM)


def fetch(sems, *copies):
    started = [pltpu.make_async_copy(a, b, sems.at[i]) for i, (a, b) in enumerate(copies)]
    for copy in started:
        copy.start()

    def wait():
        for copy in started:
            copy.wait()

    return wait


def pack_kernel(
    pos_hbm, vel_hbm, typ_hbm, counts_hbm, send_hbm, out, top, face, pos, vel, typ, counts, send, sems
):
    fetch(
        sems, (pos_hbm, pos), (vel_hbm, vel), (typ_hbm, typ), (counts_hbm, counts), (send_hbm, send)
    )()
    tiles = out.shape[0]
    width = out.shape[2]
    lane = lax.broadcasted_iota(jnp.int32, (1, width), 1)
    upper = top.shape[0]
    offsets, cap = send.shape[0], send.shape[2]
    for g in range(tiles):
        cols = pl.ds(g * width, width)
        live = lane < counts[g]
        for c in range(3):
            out[g, pl.ds(c, 1), :] = jnp.where(live, pos[pl.ds(c, 1), cols], far_away)
            out[g, pl.ds(3 + c, 1), :] = vel[pl.ds(c, 1), cols]
        out[g, pl.ds(6, 1), :] = typ[pl.ds(g, 1), :].astype(f32)
        meta = jnp.full((1, width), counts[g], jnp.int32)
        o = g - (tiles - upper)
        if 0 <= o < offsets:
            for c in range(cap):
                meta = jnp.where(lane == c, send[o, 0, c], meta)
        out[g, pl.ds(7, 1), :] = meta.astype(f32)
    top[...] = out[pl.ds(tiles - upper, upper)]
    face[...] = out[pl.ds(0, face.shape[0])]


def diagonal(width):
    lane = lax.broadcasted_iota(jnp.int32, (8, width), 1)
    return lane - lax.broadcasted_iota(jnp.int32, (8, width), 0)


def spread_row(row, store):
    width = row.shape[1]
    diff = diagonal(width)
    row = jnp.broadcast_to(row, (8, width))
    for r in range(0, width, 8):
        one = jnp.sum(jnp.where(diff == r, row, 0.0), axis=1, keepdims=True)
        store(r, jnp.broadcast_to(one, (8, width)))


def row_sums(acc, *at):
    width = acc.shape[-1]
    diff = diagonal(width)
    out = jnp.zeros((8, width), f32)
    for r in range(0, width, 8):
        out = jnp.where(diff == r, jnp.sum(acc[*at, pl.ds(r, 8), :], axis=1, keepdims=True), out)
    return out


def by_fours(tiles, body):
    def step(i, carry):
        for t in range(4):
            body(4 * i + t)
        return carry

    lax.fori_loop(0, tiles // 4, step, 0)


def fold(ref, first, *at):
    width = ref.shape[-1]
    sub = lax.broadcasted_iota(jnp.int32, (8, width), 0)
    parts = [ref[*at, first + t] for t in range(8)]
    for step in (4, 2, 1):
        low = sub % (2 * step) < step
        parts = [
            jnp.where(low, a, b) + pltpu.roll(jnp.where(low, b, a), step, 0)
            if step == 4
            else jnp.where(low, a, b)
            + jnp.where(
                low,
                pltpu.roll(jnp.where(low, b, a), 8 - step, 0),
                pltpu.roll(jnp.where(low, b, a), step, 0),
            )
            for a, b in zip(parts[:step], parts[step:])
        ]
    return parts[0]


def branch(used, count, width, eighths, body):
    sizes = (0,) + tuple(width * e // 8 for e in eighths)
    index = jnp.where(used, 1, 0)
    for n in sizes[1:-1]:
        index += jnp.where(used & (count > n), 1, 0)

    def pick(low, high):
        if low == high:
            body(sizes[low])
            return
        middle = (low + high) // 2

        @pl.when(index <= middle)
        def _():
            pick(low, middle)

        @pl.when(index > middle)
        def _():
            pick(middle + 1, high)

    pick(0, len(sizes) - 1)


def tile_loop(tiles, width, counts, slots, eighths, partner, pair):
    def step(g, carry):
        count = counts[g]
        listed = [partner(g, k) for k in range(slots)]
        for k, (h, used) in enumerate(listed):

            def body(n, k=k, h=h):
                if n:
                    pair(g, k, h, n)

            branch(used & (count > 0), count, width, eighths, body)
        return carry

    lax.fori_loop(0, tiles, step, 0)


def column(ref, h, c):
    return jnp.broadcast_to(ref[h, pl.ds(c, 1), :], (8, ref.shape[2]))


def density_pair(mine, union, h, n, acc_cols, acc_rows, g):
    other = [column(union, h, c) for c in range(3)]
    total = None
    for r in range(0, n, 8):
        d = [mine(c, r) - other[c] for c in range(3)]
        d2 = jnp.maximum(d[0] * d[0] + d[1] * d[1] + d[2] * d[2], distance_floor)
        w = jnp.maximum(cutoff_density - d2 * lax.rsqrt(d2), 0.0)
        w = w * w
        total = w if total is None else total + w
        if acc_rows is not None:
            acc_rows[g, pl.ds(r, 8), :] += w
    acc_cols[h] += total


def force_pair(mine, union, h, n, table, acc_cols, acc_rows, g):
    a00, a01, a11 = table
    other = [column(union, h, c) for c in range(8)]
    first = a00 + other[6] * (a01 - a00)
    slope = (a01 + other[6] * (a11 - a01)) - first
    total = [None] * 3
    for r in range(0, n, 8):
        d = [mine(c, r) - other[c] for c in range(3)]
        d2 = jnp.maximum(d[0] * d[0] + d[1] * d[1] + d[2] * d[2], distance_floor)
        inverse = lax.rsqrt(d2)
        dist = d2 * inverse
        wc = jnp.maximum(1.0 - dist, 0.0)
        wd = jnp.maximum(cutoff_density - dist, 0.0)
        dv = [mine(3 + c, r) - other[3 + c] for c in range(3)]
        approach = (d[0] * dv[0] + d[1] * dv[1] + d[2] * dv[2]) * inverse
        scalar = (first + mine(6, r) * slope) - approach * wc
        scalar = scalar * wc + (mine(7, r) + other[7]) * wd
        scalar = scalar * inverse
        for c in range(3):
            push = d[c] * scalar
            total[c] = push if total[c] is None else total[c] + push
            if acc_rows is not None:
                acc_rows[c, g, pl.ds(r, 8), :] += push
    for c in range(3):
        acc_cols[c, h] -= total[c]


def zero(*refs):
    for ref in refs:
        ref[...] = jnp.zeros_like(ref)


def spread_kernel(union, spread, token):
    tiles = union.shape[0]
    zero(token)

    def fill(g):
        for c in range(spread.shape[1]):

            def store(r, value, c=c):
                spread[g, c, pl.ds(r, 8), :] = value

            row = union[g, pl.ds(c, 1), :]
            spread_row(row * friction if 3 <= c < 6 else row, store)

    by_fours(tiles, fill)


def local_partner(counts, nbr):
    def partner(g, k):
        if k == 0:
            return g, True
        h = nbr[k - 1, g]
        return jnp.maximum(h, 0), (h >= 0) & (counts[jnp.maximum(h, 0)] > 0)

    return partner


def local_density_kernel(counts_hbm, nbr_hbm, union, spread, acc, sums, counts, nbr, sems):
    wait = fetch(sems, (counts_hbm, counts), (nbr_hbm, nbr))
    tiles, width = union.shape[0], union.shape[2]
    zero(sums)
    wait()
    self_term = (cutoff_density - math.sqrt(distance_floor)) ** 2
    lane = lax.broadcasted_iota(jnp.int32, (8, width), 1)
    sub = lax.broadcasted_iota(jnp.int32, (8, width), 0)
    for g in range(tiles):
        acc[g] = jnp.where((lane < counts[g]) & (sub == 0), -self_term, 0.0)

    def pair(g, k, h, n):
        mine = lambda c, r: spread[g, c, pl.ds(r, 8), :]
        density_pair(mine, union, h, n, acc, sums if k else None, g)

    tile_loop(
        tiles, width, counts, 1 + nbr.shape[0], DENSITY_SIZES, local_partner(counts, nbr), pair
    )


def gather(target, *refs):
    at = 0
    for ref in refs:
        target[pl.ds(at, ref.shape[0])] = ref[...]
        at += ref.shape[0]


def spill(target, at, *refs):
    for ref in refs:
        ref[...] = target[pl.ds(at, ref.shape[0])]
        at += ref.shape[0]


def ghost_meta(ghosts, meta, meta_smem, sem):
    total = ghosts.shape[0]
    for t in range(total):
        meta[pl.ds(t, 1), :] = ghosts[t, pl.ds(7, 1), :].astype(jnp.int32)
    copy = pltpu.make_async_copy(meta, meta_smem, sem)
    copy.start()
    return copy.wait


def ghost_partner(k, g, face_nbr, cross_pair, where, meta, faces, upper, cap, reach):
    columns = face_nbr.shape[0]
    if k < columns:
        f = face_nbr[k, g]
        h = jnp.maximum(f, 0)
        return h, (f >= 0) & (meta[h, meta.shape[1] - 1] > 0)
    s = cross_pair[k - columns, g]
    layer, core = where[0], where[1]
    slot = jnp.maximum(s, 0)
    o = slot // cap
    c = slot - o * cap
    place = core - o + 2 * reach
    hop = place // 2 - 1
    flipped = jnp.where(lax.rem(place, 2) == core, 0, 1)
    hops = jnp.where(hop == 0, 0, jnp.where(hop < 0, 1, 2))
    base = faces + (hops * 2 + flipped) * upper
    u = meta[base + o, c]
    h = base + jnp.maximum(u, 0)
    return h, (s >= 0) & (layer > 0) & (u >= 0) & (meta[h, meta.shape[1] - 1] > 0)


def ghost_density_kernel(
    faces,
    upper,
    cap,
    reach,
    where,
    counts_hbm,
    face_nbr_hbm,
    cross_pair_hbm,
    spread,
    local_acc,
    local_sums,
    face,
    near,
    flip,
    below,
    above,
    own_out,
    top_out,
    face_out,
    pair_out,
    below_out,
    above_out,
    sums,
    listed,
    ghosts,
    acc,
    reduced,
    counts,
    face_nbr,
    cross_pair,
    meta,
    meta_smem,
    sems,
    sem,
):
    wait = fetch(
        sems, (counts_hbm, counts), (face_nbr_hbm, face_nbr), (cross_pair_hbm, cross_pair)
    )
    tiles, width = spread.shape[0], spread.shape[2]
    gather(ghosts, face, near, flip, below, above)
    wait_meta = ghost_meta(ghosts, meta, meta_smem, sem)
    wait()
    wait_meta()
    zero(acc)
    slots = face_nbr.shape[0] + cross_pair.shape[0]
    for g in range(tiles):
        for k in range(slots):
            h, ok = ghost_partner(
                k, g, face_nbr, cross_pair, where, meta_smem, faces, upper, cap, reach
            )
            listed[k, g] = jnp.where(ok & (counts[g] > 0), h, -1)

    def partner(g, k):
        h = listed[k, g]
        return jnp.maximum(h, 0), h >= 0

    def pair(g, k, h, n):
        mine = lambda c, r: spread[g, c, pl.ds(r, 8), :]
        density_pair(mine, ghosts, h, n, acc, sums, g)

    tile_loop(tiles, width, counts, slots, DENSITY_SIZES, partner, pair)
    for t in range(0, acc.shape[0], 8):
        reduced[pl.ds(t, 8), :] = fold(acc, t)
    face_out[...] = reduced[pl.ds(0, faces)]
    spill(reduced, faces, pair_out)
    below_out[pl.ds(0, 2 * upper)] = reduced[pl.ds(faces + 2 * upper, 2 * upper)]
    below_out[pl.ds(2 * upper, faces)] = reduced[pl.ds(0, faces)]
    spill(reduced, faces + 4 * upper, above_out)

    def collect(t):
        acc[t] = local_acc[t] + row_sums(sums, t)

    by_fours(tiles, collect)
    for t in range(0, tiles, 8):
        own_out[pl.ds(t, 8), :] = fold(acc, t)
    top_out[...] = own_out[pl.ds(tiles - upper, upper)]


def force_tile(union, density, t):
    tile = union[t]
    channel = lax.broadcasted_iota(jnp.int32, tile.shape, 0)
    tile = jnp.where((channel >= 3) & (channel < 6), tile * friction, tile)
    return jnp.where(channel == 7, density * (crowd_scale * density_scale), tile)


def amplitudes(a_table):
    return (a_table[0, 0], 0.5 * (a_table[0, 1] + a_table[1, 0]), a_table[1, 1])


def force_mine(spread, crowd, g):
    def mine(c, r):
        return crowd[g, pl.ds(r, 8), :] if c == 7 else spread[g, c, pl.ds(r, 8), :]

    return mine


def listed_partner(listed, first, shift):
    def partner(g, k):
        h = listed[first + k, g]
        return jnp.maximum(h - shift, 0), h >= 0

    return partner


def cross_force_kernel(
    columns,
    faces,
    counts_hbm,
    listed_hbm,
    a_table,
    spread,
    density,
    near,
    flip,
    below,
    above,
    pair_rho,
    below_rho,
    above_rho,
    crowd,
    sums,
    pair_out,
    below_out,
    above_out,
    ghosts,
    acc,
    rho,
    reduced,
    counts,
    listed,
    sems,
):
    wait = fetch(sems, (counts_hbm, counts), (listed_hbm, listed))
    tiles, width = spread.shape[0], spread.shape[2]
    zero(acc, sums)
    table = amplitudes(a_table)
    gather(ghosts, near, flip, below, above)
    gather(rho, pair_rho, below_rho, above_rho)
    for t in range(ghosts.shape[0]):
        ghosts[t] = force_tile(ghosts, rho[pl.ds(t, 1), :], t)

    def fill(g):
        def store(r, value):
            crowd[g, pl.ds(r, 8), :] = value

        spread_row(density[pl.ds(g, 1), :] * (crowd_scale * density_scale), store)

    by_fours(tiles, fill)
    wait()

    def pair(g, k, h, n):
        force_pair(force_mine(spread, crowd, g), ghosts, h, n, table, acc, sums, g)

    partner = listed_partner(listed, columns, faces)
    tile_loop(tiles, width, counts, listed.shape[0] - columns, FORCE_SIZES, partner, pair)
    for c in range(3):
        for t in range(0, acc.shape[1], 8):
            reduced[pl.ds(t, 8), :] = fold(acc, t, c)
        spill(reduced, 0, pair_out.at[c], below_out.at[c], above_out.at[c])


def face_force_kernel(
    columns,
    counts_hbm,
    listed_hbm,
    a_table,
    spread,
    crowd,
    cross_sums,
    face,
    face_rho,
    sums,
    face_out,
    ghosts,
    acc,
    counts,
    listed,
    sems,
):
    wait = fetch(sems, (counts_hbm, counts), (listed_hbm, listed))
    tiles, width = spread.shape[0], spread.shape[2]
    zero(acc)
    sums[...] = cross_sums[...]
    table = amplitudes(a_table)
    for t in range(ghosts.shape[0]):
        ghosts[t] = force_tile(face, face_rho[pl.ds(t, 1), :], t)
    wait()

    def pair(g, k, h, n):
        force_pair(force_mine(spread, crowd, g), ghosts, h, n, table, acc, sums, g)

    tile_loop(tiles, width, counts, columns, FORCE_SIZES, listed_partner(listed, 0, 0), pair)
    for c in range(3):
        for t in range(0, acc.shape[1], 8):
            face_out[c, pl.ds(t, 8), :] = fold(acc, t, c)


def local_force_kernel(
    counts_hbm,
    nbr_hbm,
    a_table,
    union,
    spread,
    crowd,
    density,
    ghost_sums,
    acc,
    beads,
    sums,
    counts,
    nbr,
    sems,
):
    wait = fetch(sems, (counts_hbm, counts), (nbr_hbm, nbr))
    tiles, width = union.shape[0], union.shape[2]
    table = amplitudes(a_table)
    zero(acc)
    sums[...] = ghost_sums[...]
    for t in range(tiles):
        beads[t] = force_tile(union, density[pl.ds(t, 1), :], t)
    wait()

    def pair(g, k, h, n):
        force_pair(force_mine(spread, crowd, g), beads, h, n, table, acc, sums if k else None, g)

    tile_loop(
        tiles, width, counts, 1 + nbr.shape[0], FORCE_SIZES, local_partner(counts, nbr), pair
    )

    def collect(t):
        for c in range(3):
            acc[c, t] += row_sums(sums, c, t)

    by_fours(tiles, collect)


def finish_kernel(counts, pos, vel, acc, face_back, top_back, pos_out, vel_out):
    tiles, width = acc.shape[1], acc.shape[3]
    faces, upper = face_back.shape[1], top_back.shape[1]
    lane = lax.broadcasted_iota(jnp.int32, (1, width), 1)
    for c in range(3):
        for t in range(0, tiles, 8):
            total = fold(acc, t, c)
            if t < faces:
                total = total + face_back[c, pl.ds(t, 8), :]
            if t >= tiles - upper:
                total = total + top_back[c, pl.ds(t - (tiles - upper), 8), :]
            for i in range(8):
                g = t + i
                cols = pl.ds(g * width, width)
                live = lane < counts[g]
                speed = vel[pl.ds(c, 1), cols] + time_step * total[i : i + 1]
                speed = jnp.where(live, speed, 0.0)
                vel_out[pl.ds(c, 1), cols] = speed
                place = jnp.where(live, pos[pl.ds(c, 1), cols] + time_step * speed, 0.0)
                pos_out[pl.ds(c, 1), cols] = place


def on_device(
    layers,
    places,
    positions,
    velocities,
    types,
    counts,
    a_table,
    local_nbr,
    face_nbr,
    cross_send,
    cross_pair,
):
    tiles = counts.shape[0]
    width = positions.shape[1] // tiles
    faces, upper = tiles // 4, tiles // 2
    offsets, cap = cross_send.shape[1], cross_send.shape[2]
    reach = offsets // 2
    total = faces + 6 * upper
    both = ("layer", "lat")

    def lateral(value, by):
        return lax.ppermute(value, "lat", [(m, (m + by) % places) for m in range(places)])

    def swap(value):
        return lax.ppermute(value, "lat", [(m, m ^ 1) for m in range(places)])

    def climb(value, by, flip=0):
        return lax.ppermute(
            value,
            both,
            [
                (l * places + m, ((l + by) % layers) * places + (m ^ flip))
                for l in range(layers)
                for m in range(places)
            ],
        )

    kinds = types.reshape(tiles, width)
    local_nbr, face_nbr, cross_pair = (
        in_hbm(table.T) for table in (local_nbr, face_nbr, cross_pair)
    )
    send = in_hbm(cross_send.transpose(1, 0, 2))
    counts_hbm = in_hbm(counts)
    ints = jnp.int32
    counts_smem = pltpu.SMEM((tiles,), ints)
    payload, top, face = pl.pallas_call(
        pack_kernel,
        out_shape=(sds(tiles, 8, width), sds(upper, 8, width), sds(faces, 8, width)),
        in_specs=[HBM] * 5,
        out_specs=[VMEM] * 3,
        scratch_shapes=[
            pltpu.VMEM(positions.shape, f32),
            pltpu.VMEM(velocities.shape, f32),
            pltpu.VMEM(kinds.shape, ints),
            counts_smem,
            pltpu.SMEM(send.shape, ints),
            pltpu.SemaphoreType.DMA((5,)),
        ],
        compiler_params=params(),
    )(in_hbm(positions), in_hbm(velocities), in_hbm(kinds), counts_hbm, send)
    near = climb(top, 1)
    flip = climb(top, 1, 1)
    face_ghosts = lateral(face, 1)
    def spread_rows(payload, channels):
        return pl.pallas_call(
            spread_kernel,
            out_shape=(sds(tiles, channels, width, width), sds(8, width)),
            in_specs=[VMEM],
            out_specs=[VMEM] * 2,
            cost_estimate=pl.CostEstimate(
                flops=10**9, bytes_accessed=15 * 10**6, transcendentals=0
            ),
            compiler_params=params(),
        )(payload)

    near = climb(top, 1)
    flip = climb(top, 1, 1)
    face_ghosts = lateral(face, 1)
    spread, token = spread_rows(payload, 3)
    near, flip, spread = lax.optimization_barrier((near, flip, spread))
    chip_ghosts = jnp.concatenate([near, flip], axis=0)
    below = lateral(chip_ghosts, 2)
    above = lateral(chip_ghosts, -2)
    where = jnp.stack([lax.axis_index("layer"), lax.axis_index("lat") % 2]).astype(jnp.int32)

    local_acc, local_sums = pl.pallas_call(
        local_density_kernel,
        out_shape=(sds(tiles, 8, width), sds(tiles, width, width)),
        in_specs=[HBM, HBM, VMEM, VMEM],
        out_specs=[VMEM] * 2,
        scratch_shapes=[
            counts_smem,
            pltpu.SMEM(local_nbr.shape, ints),
            pltpu.SemaphoreType.DMA((2,)),
        ],
        cost_estimate=pl.CostEstimate(flops=10**9, bytes_accessed=15 * 10**6, transcendentals=0),
        compiler_params=params(),
    )(counts_hbm, local_nbr, payload, spread)

    sizes = (faces, upper, cap, reach)
    tables = [
        counts_smem,
        pltpu.SMEM(face_nbr.shape, ints),
        pltpu.SMEM(cross_pair.shape, ints),
        pltpu.VMEM((total, width), ints),
        pltpu.SMEM((total, width), ints),
        pltpu.SemaphoreType.DMA((3,)),
        pltpu.SemaphoreType.DMA,
    ]
    own, own_top, face_part, pair_part, below_part, above_part, _, listed = pl.pallas_call(
        functools.partial(ghost_density_kernel, *sizes),
        out_shape=(
            sds(tiles, width),
            sds(upper, width),
            sds(faces, width),
            sds(2 * upper, width),
            sds(2 * upper + faces, width),
            sds(2 * upper, width),
            sds(tiles, width, width),
            jax.ShapeDtypeStruct((face_nbr.shape[0] + cross_pair.shape[0], tiles), ints),
        ),
        in_specs=[SMEM] + [HBM] * 3 + [VMEM] * 8,
        out_specs=[VMEM] * 7 + [SMEM],
        scratch_shapes=[
            pltpu.VMEM((total, 8, width), f32),
            pltpu.VMEM((total, 8, width), f32),
            pltpu.VMEM((total, width), f32),
        ]
        + tables,
        input_output_aliases={6: 6},
        compiler_params=params(),
    )(
        where,
        counts_hbm,
        face_nbr,
        cross_pair,
        spread,
        local_acc,
        local_sums,
        face_ghosts,
        near,
        flip,
        below,
        above,
    )

    pairs = 2 * upper
    odd = where[1] == 1
    owner_part = climb(own_top, 1)
    from_above = lateral(below_part, -2)
    from_below = lateral(above_part, 2)
    payload, _ = lax.optimization_barrier((payload, pair_part))
    spread, token = spread_rows(payload, 7)
    passed = jnp.where(odd, face_part, from_above[pairs:])
    met = pair_part + from_above[:pairs] + from_below
    met = jnp.concatenate([met[:upper] + owner_part, met[upper:]], axis=0)
    other = swap(jnp.concatenate([met, passed, own[:faces]], axis=0))
    other, spread = lax.optimization_barrier((other, spread))
    pair_rho = met + jnp.concatenate([other[upper:pairs], other[:upper]], axis=0)
    bottom_rho = own[:faces] + other[pairs : pairs + faces]
    other_rho = passed + other[pairs + faces :]
    top_rho = climb(pair_rho[:upper], -1)
    below_rho = lateral(jnp.concatenate([pair_rho, other_rho], axis=0), 2)
    above_rho = lateral(pair_rho, -2)
    face_rho = jnp.where(odd, other_rho, below_rho[pairs:])
    below_rho = below_rho[:pairs]
    density = jnp.concatenate([bottom_rho, own[faces : tiles - upper], top_rho], axis=0)

    columns = face_nbr.shape[0]
    small = [
        counts_smem,
        pltpu.SMEM(listed.shape, ints),
        pltpu.SemaphoreType.DMA((2,)),
    ]
    crowd, cross_sums, pair_force, below_force, above_force = pl.pallas_call(
        functools.partial(cross_force_kernel, columns, faces),
        out_shape=(
            sds(tiles, width, width),
            sds(3, tiles, width, width),
            sds(3, pairs, width),
            sds(3, pairs, width),
            sds(3, pairs, width),
        ),
        in_specs=[HBM] * 2 + [SMEM] + [VMEM] * 9,
        out_specs=[VMEM] * 5,
        scratch_shapes=[
            pltpu.VMEM((3 * pairs, 8, width), f32),
            pltpu.VMEM((3, 3 * pairs, 8, width), f32),
            pltpu.VMEM((3 * pairs, width), f32),
            pltpu.VMEM((3 * pairs, width), f32),
        ]
        + small,
        compiler_params=params(),
    )(
        counts_hbm,
        listed,
        a_table,
        spread,
        density,
        near,
        flip,
        below,
        above,
        pair_rho,
        below_rho,
        above_rho,
    )
    from_above = lateral(below_force, -2)
    from_below = lateral(above_force, 2)
    ghost_sums, face_force = pl.pallas_call(
        functools.partial(face_force_kernel, columns),
        out_shape=(sds(3, tiles, width, width), sds(3, faces, width)),
        in_specs=[HBM] * 2 + [SMEM] + [VMEM] * 5,
        out_specs=[VMEM] * 2,
        scratch_shapes=[
            pltpu.VMEM((faces, 8, width), f32),
            pltpu.VMEM((3, faces, 8, width), f32),
        ]
        + small,
        cost_estimate=pl.CostEstimate(flops=10**9, bytes_accessed=20 * 10**6, transcendentals=0),
        compiler_params=params(),
    )(counts_hbm, listed, a_table, spread, crowd, cross_sums, face_ghosts, face_rho)
    from_above, from_below, face_force = lax.optimization_barrier(
        (from_above, from_below, face_force)
    )
    force_face = lateral(face_force, -1)
    force_met = pair_force + from_above + from_below
    force_other = swap(force_met[:, upper:])
    force_top = climb(force_met[:, :upper] + force_other, -1)

    force = pl.pallas_call(
        local_force_kernel,
        out_shape=sds(3, tiles, 8, width),
        in_specs=[HBM, HBM, SMEM] + [VMEM] * 5,
        out_specs=VMEM,
        scratch_shapes=[
            pltpu.VMEM((tiles, 8, width), f32),
            pltpu.VMEM((3, tiles, width, width), f32),
            counts_smem,
            pltpu.SMEM(local_nbr.shape, ints),
            pltpu.SemaphoreType.DMA((2,)),
        ],
        cost_estimate=pl.CostEstimate(flops=2 * 10**9, bytes_accessed=20 * 10**6, transcendentals=0),
        compiler_params=params(),
    )(counts_hbm, local_nbr, a_table, payload, spread, crowd, density, ghost_sums)

    return pl.pallas_call(
        finish_kernel,
        out_shape=(sds(*positions.shape), sds(*velocities.shape)),
        in_specs=[SMEM] + [VMEM] * 5,
        out_specs=[VMEM] * 2,
        compiler_params=params(),
    )(counts, positions, velocities, force, force_face, force_top)


def solution(mesh):
    placed = (
        P(None, ("layer", "lat")),
        P(None, ("layer", "lat")),
        P(("layer", "lat")),
        P(("layer", "lat")),
        P(),
        P(("layer", "lat"), None),
        P(("layer", "lat"), None),
        P(("layer", "lat"), None, None),
        P(("layer", "lat"), None),
    )
    return jax.shard_map(
        functools.partial(on_device, mesh.shape["layer"], mesh.shape["lat"]),
        mesh=mesh,
        in_specs=placed,
        out_specs=(P(None, ("layer", "lat")), P(None, ("layer", "lat"))),
        check_vma=False,
    )
```

```python
import functools
import math

import jax
import jax.numpy as jnp
from jax import lax
from jax.experimental import pallas as pl
from jax.experimental.pallas import tpu as pltpu
from jax.sharding import PartitionSpec as P

cutoff_density = 0.75
density_norm = 15.0 / (2.0 * math.pi * cutoff_density**3)
repulse = 25.0
friction = 4.5
time_step = 0.01
distance_floor = 0.01
far_away = 10000.0
DENSITY_SIZES = (8,)
FORCE_SIZES = (5, 8)
density_scale = density_norm / (cutoff_density * cutoff_density)
crowd_scale = repulse / cutoff_density
VMEM = pl.BlockSpec(memory_space=pltpu.VMEM)
SMEM = pl.BlockSpec(memory_space=pltpu.SMEM)
HBM = pl.BlockSpec(memory_space=pltpu.HBM)
f32 = jnp.float32


def sds(*shape):
    return jax.ShapeDtypeStruct(shape, f32)


def params(mib=16):
    return pltpu.CompilerParams(vmem_limit_bytes=mib * 1024 * 1024)


def in_hbm(value):
    return pltpu.with_memory_space_constraint(value, pltpu.HBM)


def fetch(sems, *copies):
    started = [pltpu.make_async_copy(a, b, sems.at[i]) for i, (a, b) in enumerate(copies)]
    for copy in started:
        copy.start()

    def wait():
        for copy in started:
            copy.wait()

    return wait


def pack_kernel(
    pos_hbm, vel_hbm, typ_hbm, counts_hbm, send_hbm, out, top, face, pos, vel, typ, counts, send, sems
):
    fetch(
        sems, (pos_hbm, pos), (vel_hbm, vel), (typ_hbm, typ), (counts_hbm, counts), (send_hbm, send)
    )()
    tiles = out.shape[0]
    width = out.shape[2]
    lane = lax.broadcasted_iota(jnp.int32, (1, width), 1)
    upper = top.shape[0]
    offsets, cap = send.shape[0], send.shape[2]
    for g in range(tiles):
        cols = pl.ds(g * width, width)
        live = lane < counts[g]
        for c in range(3):
            out[g, pl.ds(c, 1), :] = jnp.where(live, pos[pl.ds(c, 1), cols], far_away)
            out[g, pl.ds(3 + c, 1), :] = vel[pl.ds(c, 1), cols]
        out[g, pl.ds(6, 1), :] = typ[pl.ds(g, 1), :].astype(f32)
        meta = jnp.full((1, width), counts[g], jnp.int32)
        o = g - (tiles - upper)
        if 0 <= o < offsets:
            for c in range(cap):
                meta = jnp.where(lane == c, send[o, 0, c], meta)
        out[g, pl.ds(7, 1), :] = meta.astype(f32)
    top[...] = out[pl.ds(tiles - upper, upper)]
    face[...] = out[pl.ds(0, face.shape[0])]


def diagonal(width):
    lane = lax.broadcasted_iota(jnp.int32, (8, width), 1)
    return lane - lax.broadcasted_iota(jnp.int32, (8, width), 0)


def spread_row(row, store):
    width = row.shape[1]
    diff = diagonal(width)
    row = jnp.broadcast_to(row, (8, width))
    for r in range(0, width, 8):
        one = jnp.sum(jnp.where(diff == r, row, 0.0), axis=1, keepdims=True)
        store(r, jnp.broadcast_to(one, (8, width)))


def row_sums(acc, *at):
    width = acc.shape[-1]
    diff = diagonal(width)
    out = jnp.zeros((8, width), f32)
    for r in range(0, width, 8):
        out = jnp.where(diff == r, jnp.sum(acc[*at, pl.ds(r, 8), :], axis=1, keepdims=True), out)
    return out


def by_eights(tiles, body):
    def step(i, carry):
        for t in range(8):
            body(8 * i + t)
        return carry

    lax.fori_loop(0, tiles // 8, step, 0)


def fold(ref, first, *at):
    width = ref.shape[-1]
    sub = lax.broadcasted_iota(jnp.int32, (8, width), 0)
    parts = [ref[*at, first + t] for t in range(8)]
    for step in (4, 2, 1):
        low = sub % (2 * step) < step
        parts = [
            jnp.where(low, a, b) + pltpu.roll(jnp.where(low, b, a), step, 0)
            if step == 4
            else jnp.where(low, a, b)
            + jnp.where(
                low,
                pltpu.roll(jnp.where(low, b, a), 8 - step, 0),
                pltpu.roll(jnp.where(low, b, a), step, 0),
            )
            for a, b in zip(parts[:step], parts[step:])
        ]
    return parts[0]


def branch(used, count, width, eighths, body):
    sizes = (0,) + tuple(width * e // 8 for e in eighths)
    index = jnp.where(used, 1, 0)
    for n in sizes[1:-1]:
        index += jnp.where(used & (count > n), 1, 0)

    def pick(low, high):
        if low == high:
            body(sizes[low])
            return
        middle = (low + high) // 2

        @pl.when(index <= middle)
        def _():
            pick(low, middle)

        @pl.when(index > middle)
        def _():
            pick(middle + 1, high)

    pick(0, len(sizes) - 1)


def tile_loop(tiles, width, counts, slots, eighths, partner, pair):
    def step(g, carry):
        count = counts[g]
        listed = [partner(g, k) for k in range(slots)]
        for k, (h, used) in enumerate(listed):

            def body(n, k=k, h=h):
                if n:
                    pair(g, k, h, n)

            branch(used & (count > 0), count, width, eighths, body)
        return carry

    lax.fori_loop(0, tiles, step, 0)


def column(ref, h, c):
    return jnp.broadcast_to(ref[h, pl.ds(c, 1), :], (8, ref.shape[2]))


def density_pair(mine, union, h, n, acc_cols, acc_rows, g):
    other = [column(union, h, c) for c in range(3)]
    total = None
    for r in range(0, n, 8):
        d = [mine(c, r) - other[c] for c in range(3)]
        d2 = jnp.maximum(d[0] * d[0] + d[1] * d[1] + d[2] * d[2], distance_floor)
        w = jnp.maximum(cutoff_density - d2 * lax.rsqrt(d2), 0.0)
        w = w * w
        total = w if total is None else total + w
        if acc_rows is not None:
            acc_rows[g, pl.ds(r, 8), :] += w
    acc_cols[h] += total


def force_pair(mine, union, h, n, table, acc_cols, acc_rows, g):
    a00, a01, a11 = table
    other = [column(union, h, c) for c in range(8)]
    first = a00 + other[6] * (a01 - a00)
    slope = (a01 + other[6] * (a11 - a01)) - first
    total = [None] * 3
    for r in range(0, n, 8):
        d = [mine(c, r) - other[c] for c in range(3)]
        d2 = jnp.maximum(d[0] * d[0] + d[1] * d[1] + d[2] * d[2], distance_floor)
        inverse = lax.rsqrt(d2)
        dist = d2 * inverse
        wc = jnp.maximum(1.0 - dist, 0.0)
        wd = jnp.maximum(cutoff_density - dist, 0.0)
        dv = [mine(3 + c, r) - other[3 + c] for c in range(3)]
        approach = (d[0] * dv[0] + d[1] * dv[1] + d[2] * dv[2]) * inverse
        scalar = (first + mine(6, r) * slope) - approach * wc
        scalar = scalar * wc + (mine(7, r) + other[7]) * wd
        scalar = scalar * inverse
        for c in range(3):
            push = d[c] * scalar
            total[c] = push if total[c] is None else total[c] + push
            if acc_rows is not None:
                acc_rows[c, g, pl.ds(r, 8), :] += push
    for c in range(3):
        acc_cols[c, h] -= total[c]


def zero(*refs):
    for ref in refs:
        ref[...] = jnp.zeros_like(ref)


def spread_kernel(union, spread, token):
    tiles = union.shape[0]
    zero(token)

    def fill(g):
        for c in range(spread.shape[1]):

            def store(r, value, c=c):
                spread[g, c, pl.ds(r, 8), :] = value

            row = union[g, pl.ds(c, 1), :]
            spread_row(row * friction if 3 <= c < 6 else row, store)

    by_eights(tiles, fill)


def local_partner(counts, nbr):
    def partner(g, k):
        if k == 0:
            return g, True
        h = nbr[k - 1, g]
        return jnp.maximum(h, 0), (h >= 0) & (counts[jnp.maximum(h, 0)] > 0)

    return partner


def local_density_kernel(counts_hbm, nbr_hbm, union, spread, acc, sums, counts, nbr, sems):
    wait = fetch(sems, (counts_hbm, counts), (nbr_hbm, nbr))
    tiles, width = union.shape[0], union.shape[2]
    zero(sums)
    wait()
    self_term = (cutoff_density - math.sqrt(distance_floor)) ** 2
    lane = lax.broadcasted_iota(jnp.int32, (8, width), 1)
    sub = lax.broadcasted_iota(jnp.int32, (8, width), 0)
    for g in range(tiles):
        acc[g] = jnp.where((lane < counts[g]) & (sub == 0), -self_term, 0.0)

    def pair(g, k, h, n):
        mine = lambda c, r: spread[g, c, pl.ds(r, 8), :]
        density_pair(mine, union, h, n, acc, sums if k else None, g)

    tile_loop(
        tiles, width, counts, 1 + nbr.shape[0], DENSITY_SIZES, local_partner(counts, nbr), pair
    )


def gather(target, *refs):
    at = 0
    for ref in refs:
        target[pl.ds(at, ref.shape[0])] = ref[...]
        at += ref.shape[0]


def spill(target, at, *refs):
    for ref in refs:
        ref[...] = target[pl.ds(at, ref.shape[0])]
        at += ref.shape[0]


def ghost_meta(ghosts, meta, meta_smem, sem):
    total = ghosts.shape[0]
    for t in range(total):
        meta[pl.ds(t, 1), :] = ghosts[t, pl.ds(7, 1), :].astype(jnp.int32)
    copy = pltpu.make_async_copy(meta, meta_smem, sem)
    copy.start()
    return copy.wait


def ghost_partner(k, g, face_nbr, cross_pair, where, meta, faces, upper, cap, reach):
    columns = face_nbr.shape[0]
    if k < columns:
        f = face_nbr[k, g]
        h = jnp.maximum(f, 0)
        return h, (f >= 0) & (meta[h, meta.shape[1] - 1] > 0)
    s = cross_pair[k - columns, g]
    layer, core = where[0], where[1]
    slot = jnp.maximum(s, 0)
    o = slot // cap
    c = slot - o * cap
    place = core - o + 2 * reach
    hop = place // 2 - 1
    flipped = jnp.where(lax.rem(place, 2) == core, 0, 1)
    hops = jnp.where(hop == 0, 0, jnp.where(hop < 0, 1, 2))
    base = faces + (hops * 2 + flipped) * upper
    u = meta[base + o, c]
    h = base + jnp.maximum(u, 0)
    return h, (s >= 0) & (layer > 0) & (u >= 0) & (meta[h, meta.shape[1] - 1] > 0)


def ghost_density_kernel(
    faces,
    upper,
    cap,
    reach,
    where,
    counts_hbm,
    face_nbr_hbm,
    cross_pair_hbm,
    spread,
    local_acc,
    local_sums,
    face,
    near,
    flip,
    below,
    above,
    own_out,
    top_out,
    face_out,
    pair_out,
    below_out,
    above_out,
    sums,
    listed,
    ghosts,
    acc,
    reduced,
    counts,
    face_nbr,
    cross_pair,
    meta,
    meta_smem,
    sems,
    sem,
):
    wait = fetch(
        sems, (counts_hbm, counts), (face_nbr_hbm, face_nbr), (cross_pair_hbm, cross_pair)
    )
    tiles, width = spread.shape[0], spread.shape[2]
    gather(ghosts, face, near, flip, below, above)
    wait_meta = ghost_meta(ghosts, meta, meta_smem, sem)
    wait()
    wait_meta()
    zero(acc)
    slots = face_nbr.shape[0] + cross_pair.shape[0]
    for g in range(tiles):
        for k in range(slots):
            h, ok = ghost_partner(
                k, g, face_nbr, cross_pair, where, meta_smem, faces, upper, cap, reach
            )
            listed[k, g] = jnp.where(ok & (counts[g] > 0), h, -1)

    def partner(g, k):
        h = listed[k, g]
        return jnp.maximum(h, 0), h >= 0

    def pair(g, k, h, n):
        mine = lambda c, r: spread[g, c, pl.ds(r, 8), :]
        density_pair(mine, ghosts, h, n, acc, sums, g)

    tile_loop(tiles, width, counts, slots, DENSITY_SIZES, partner, pair)
    for t in range(0, acc.shape[0], 8):
        reduced[pl.ds(t, 8), :] = fold(acc, t)
    face_out[...] = reduced[pl.ds(0, faces)]
    spill(reduced, faces, pair_out)
    below_out[pl.ds(0, 2 * upper)] = reduced[pl.ds(faces + 2 * upper, 2 * upper)]
    below_out[pl.ds(2 * upper, faces)] = reduced[pl.ds(0, faces)]
    spill(reduced, faces + 4 * upper, above_out)

    def collect(t):
        acc[t] = local_acc[t] + row_sums(sums, t)

    by_eights(tiles, collect)
    for t in range(0, tiles, 8):
        own_out[pl.ds(t, 8), :] = fold(acc, t)
    top_out[...] = own_out[pl.ds(tiles - upper, upper)]


def force_tile(union, density, t):
    tile = union[t]
    channel = lax.broadcasted_iota(jnp.int32, tile.shape, 0)
    tile = jnp.where((channel >= 3) & (channel < 6), tile * friction, tile)
    return jnp.where(channel == 7, density * (crowd_scale * density_scale), tile)


def amplitudes(a_table):
    return (a_table[0, 0], 0.5 * (a_table[0, 1] + a_table[1, 0]), a_table[1, 1])


def force_mine(spread, crowd, g):
    def mine(c, r):
        return crowd[g, pl.ds(r, 8), :] if c == 7 else spread[g, c, pl.ds(r, 8), :]

    return mine


def listed_partner(listed, first, shift):
    def partner(g, k):
        h = listed[first + k, g]
        return jnp.maximum(h - shift, 0), h >= 0

    return partner


def cross_force_kernel(
    columns,
    faces,
    counts_hbm,
    listed_hbm,
    a_table,
    spread,
    density,
    near,
    flip,
    below,
    above,
    pair_rho,
    below_rho,
    above_rho,
    crowd,
    sums,
    pair_out,
    below_out,
    above_out,
    ghosts,
    acc,
    rho,
    reduced,
    counts,
    listed,
    sems,
):
    wait = fetch(sems, (counts_hbm, counts), (listed_hbm, listed))
    tiles, width = spread.shape[0], spread.shape[2]
    zero(acc, sums)
    table = amplitudes(a_table)
    gather(ghosts, near, flip, below, above)
    gather(rho, pair_rho, below_rho, above_rho)
    for t in range(ghosts.shape[0]):
        ghosts[t] = force_tile(ghosts, rho[pl.ds(t, 1), :], t)

    def fill(g):
        def store(r, value):
            crowd[g, pl.ds(r, 8), :] = value

        spread_row(density[pl.ds(g, 1), :] * (crowd_scale * density_scale), store)

    by_eights(tiles, fill)
    wait()

    def pair(g, k, h, n):
        force_pair(force_mine(spread, crowd, g), ghosts, h, n, table, acc, sums, g)

    partner = listed_partner(listed, columns, faces)
    tile_loop(tiles, width, counts, listed.shape[0] - columns, FORCE_SIZES, partner, pair)
    for c in range(3):
        for t in range(0, acc.shape[1], 8):
            reduced[pl.ds(t, 8), :] = fold(acc, t, c)
        spill(reduced, 0, pair_out.at[c], below_out.at[c], above_out.at[c])


def face_force_kernel(
    columns,
    counts_hbm,
    listed_hbm,
    a_table,
    spread,
    crowd,
    cross_sums,
    face,
    face_rho,
    sums,
    face_out,
    ghosts,
    acc,
    counts,
    listed,
    sems,
):
    wait = fetch(sems, (counts_hbm, counts), (listed_hbm, listed))
    tiles, width = spread.shape[0], spread.shape[2]
    zero(acc)
    sums[...] = cross_sums[...]
    table = amplitudes(a_table)
    for t in range(ghosts.shape[0]):
        ghosts[t] = force_tile(face, face_rho[pl.ds(t, 1), :], t)
    wait()

    def pair(g, k, h, n):
        force_pair(force_mine(spread, crowd, g), ghosts, h, n, table, acc, sums, g)

    tile_loop(tiles, width, counts, columns, FORCE_SIZES, listed_partner(listed, 0, 0), pair)
    for c in range(3):
        for t in range(0, acc.shape[1], 8):
            face_out[c, pl.ds(t, 8), :] = fold(acc, t, c)


def local_force_kernel(
    counts_hbm,
    nbr_hbm,
    a_table,
    union,
    spread,
    crowd,
    density,
    ghost_sums,
    acc,
    beads,
    sums,
    counts,
    nbr,
    sems,
):
    wait = fetch(sems, (counts_hbm, counts), (nbr_hbm, nbr))
    tiles, width = union.shape[0], union.shape[2]
    table = amplitudes(a_table)
    zero(acc)
    sums[...] = ghost_sums[...]
    for t in range(tiles):
        beads[t] = force_tile(union, density[pl.ds(t, 1), :], t)
    wait()

    def pair(g, k, h, n):
        force_pair(force_mine(spread, crowd, g), beads, h, n, table, acc, sums if k else None, g)

    tile_loop(
        tiles, width, counts, 1 + nbr.shape[0], FORCE_SIZES, local_partner(counts, nbr), pair
    )

    def collect(t):
        for c in range(3):
            acc[c, t] += row_sums(sums, c, t)

    by_eights(tiles, collect)


def finish_kernel(counts, pos, vel, acc, face_back, top_back, pos_out, vel_out):
    tiles, width = acc.shape[1], acc.shape[3]
    faces, upper = face_back.shape[1], top_back.shape[1]
    lane = lax.broadcasted_iota(jnp.int32, (1, width), 1)
    for c in range(3):
        for t in range(0, tiles, 8):
            total = fold(acc, t, c)
            if t < faces:
                total = total + face_back[c, pl.ds(t, 8), :]
            if t >= tiles - upper:
                total = total + top_back[c, pl.ds(t - (tiles - upper), 8), :]
            for i in range(8):
                g = t + i
                cols = pl.ds(g * width, width)
                live = lane < counts[g]
                speed = vel[pl.ds(c, 1), cols] + time_step * total[i : i + 1]
                speed = jnp.where(live, speed, 0.0)
                vel_out[pl.ds(c, 1), cols] = speed
                place = jnp.where(live, pos[pl.ds(c, 1), cols] + time_step * speed, 0.0)
                pos_out[pl.ds(c, 1), cols] = place


def on_device(
    layers,
    places,
    positions,
    velocities,
    types,
    counts,
    a_table,
    local_nbr,
    face_nbr,
    cross_send,
    cross_pair,
):
    tiles = counts.shape[0]
    width = positions.shape[1] // tiles
    faces, upper = tiles // 4, tiles // 2
    offsets, cap = cross_send.shape[1], cross_send.shape[2]
    reach = offsets // 2
    total = faces + 6 * upper
    both = ("layer", "lat")

    def lateral(value, by):
        return lax.ppermute(value, "lat", [(m, (m + by) % places) for m in range(places)])

    def swap(value):
        return lax.ppermute(value, "lat", [(m, m ^ 1) for m in range(places)])

    def climb(value, by, flip=0):
        return lax.ppermute(
            value,
            both,
            [
                (l * places + m, ((l + by) % layers) * places + (m ^ flip))
                for l in range(layers)
                for m in range(places)
            ],
        )

    kinds = types.reshape(tiles, width)
    local_nbr, face_nbr, cross_pair = (
        in_hbm(table.T) for table in (local_nbr, face_nbr, cross_pair)
    )
    send = in_hbm(cross_send.transpose(1, 0, 2))
    counts_hbm = in_hbm(counts)
    ints = jnp.int32
    counts_smem = pltpu.SMEM((tiles,), ints)
    payload, top, face = pl.pallas_call(
        pack_kernel,
        out_shape=(sds(tiles, 8, width), sds(upper, 8, width), sds(faces, 8, width)),
        in_specs=[HBM] * 5,
        out_specs=[VMEM] * 3,
        scratch_shapes=[
            pltpu.VMEM(positions.shape, f32),
            pltpu.VMEM(velocities.shape, f32),
            pltpu.VMEM(kinds.shape, ints),
            counts_smem,
            pltpu.SMEM(send.shape, ints),
            pltpu.SemaphoreType.DMA((5,)),
        ],
        compiler_params=params(),
    )(in_hbm(positions), in_hbm(velocities), in_hbm(kinds), counts_hbm, send)
    near = climb(top, 1)
    flip = climb(top, 1, 1)
    face_ghosts = lateral(face, 1)
    def spread_rows(payload, channels):
        return pl.pallas_call(
            spread_kernel,
            out_shape=(sds(tiles, channels, width, width), sds(8, width)),
            in_specs=[VMEM],
            out_specs=[VMEM] * 2,
            cost_estimate=pl.CostEstimate(
                flops=10**9, bytes_accessed=15 * 10**6, transcendentals=0
            ),
            compiler_params=params(),
        )(payload)

    near = climb(top, 1)
    flip = climb(top, 1, 1)
    face_ghosts = lateral(face, 1)
    spread, token = spread_rows(payload, 3)
    near, flip, spread = lax.optimization_barrier((near, flip, spread))
    chip_ghosts = jnp.concatenate([near, flip], axis=0)
    below = lateral(chip_ghosts, 2)
    above = lateral(chip_ghosts, -2)
    where = jnp.stack([lax.axis_index("layer"), lax.axis_index("lat") % 2]).astype(jnp.int32)

    local_acc, local_sums = pl.pallas_call(
        local_density_kernel,
        out_shape=(sds(tiles, 8, width), sds(tiles, width, width)),
        in_specs=[HBM, HBM, VMEM, VMEM],
        out_specs=[VMEM] * 2,
        scratch_shapes=[
            counts_smem,
            pltpu.SMEM(local_nbr.shape, ints),
            pltpu.SemaphoreType.DMA((2,)),
        ],
        cost_estimate=pl.CostEstimate(flops=10**9, bytes_accessed=15 * 10**6, transcendentals=0),
        compiler_params=params(),
    )(counts_hbm, local_nbr, payload, spread)

    sizes = (faces, upper, cap, reach)
    tables = [
        counts_smem,
        pltpu.SMEM(face_nbr.shape, ints),
        pltpu.SMEM(cross_pair.shape, ints),
        pltpu.VMEM((total, width), ints),
        pltpu.SMEM((total, width), ints),
        pltpu.SemaphoreType.DMA((3,)),
        pltpu.SemaphoreType.DMA,
    ]
    own, own_top, face_part, pair_part, below_part, above_part, _, listed = pl.pallas_call(
        functools.partial(ghost_density_kernel, *sizes),
        out_shape=(
            sds(tiles, width),
            sds(upper, width),
            sds(faces, width),
            sds(2 * upper, width),
            sds(2 * upper + faces, width),
            sds(2 * upper, width),
            sds(tiles, width, width),
            jax.ShapeDtypeStruct((face_nbr.shape[0] + cross_pair.shape[0], tiles), ints),
        ),
        in_specs=[SMEM] + [HBM] * 3 + [VMEM] * 8,
        out_specs=[VMEM] * 7 + [SMEM],
        scratch_shapes=[
            pltpu.VMEM((total, 8, width), f32),
            pltpu.VMEM((total, 8, width), f32),
            pltpu.VMEM((total, width), f32),
        ]
        + tables,
        input_output_aliases={6: 6},
        compiler_params=params(),
    )(
        where,
        counts_hbm,
        face_nbr,
        cross_pair,
        spread,
        local_acc,
        local_sums,
        face_ghosts,
        near,
        flip,
        below,
        above,
    )

    pairs = 2 * upper
    odd = where[1] == 1
    owner_part = climb(own_top, 1)
    from_above = lateral(below_part, -2)
    from_below = lateral(above_part, 2)
    payload, _ = lax.optimization_barrier((payload, pair_part))
    spread, token = spread_rows(payload, 7)
    passed = jnp.where(odd, face_part, from_above[pairs:])
    met = pair_part + from_above[:pairs] + from_below
    met = jnp.concatenate([met[:upper] + owner_part, met[upper:]], axis=0)
    other = swap(jnp.concatenate([met, passed, own[:faces]], axis=0))
    other, spread = lax.optimization_barrier((other, spread))
    pair_rho = met + jnp.concatenate([other[upper:pairs], other[:upper]], axis=0)
    bottom_rho = own[:faces] + other[pairs : pairs + faces]
    other_rho = passed + other[pairs + faces :]
    top_rho = climb(pair_rho[:upper], -1)
    below_rho = lateral(jnp.concatenate([pair_rho, other_rho], axis=0), 2)
    above_rho = lateral(pair_rho, -2)
    face_rho = jnp.where(odd, other_rho, below_rho[pairs:])
    below_rho = below_rho[:pairs]
    density = jnp.concatenate([bottom_rho, own[faces : tiles - upper], top_rho], axis=0)

    columns = face_nbr.shape[0]
    small = [
        counts_smem,
        pltpu.SMEM(listed.shape, ints),
        pltpu.SemaphoreType.DMA((2,)),
    ]
    crowd, cross_sums, pair_force, below_force, above_force = pl.pallas_call(
        functools.partial(cross_force_kernel, columns, faces),
        out_shape=(
            sds(tiles, width, width),
            sds(3, tiles, width, width),
            sds(3, pairs, width),
            sds(3, pairs, width),
            sds(3, pairs, width),
        ),
        in_specs=[HBM] * 2 + [SMEM] + [VMEM] * 9,
        out_specs=[VMEM] * 5,
        scratch_shapes=[
            pltpu.VMEM((3 * pairs, 8, width), f32),
            pltpu.VMEM((3, 3 * pairs, 8, width), f32),
            pltpu.VMEM((3 * pairs, width), f32),
            pltpu.VMEM((3 * pairs, width), f32),
        ]
        + small,
        compiler_params=params(),
    )(
        counts_hbm,
        listed,
        a_table,
        spread,
        density,
        near,
        flip,
        below,
        above,
        pair_rho,
        below_rho,
        above_rho,
    )
    from_above = lateral(below_force, -2)
    from_below = lateral(above_force, 2)
    ghost_sums, face_force = pl.pallas_call(
        functools.partial(face_force_kernel, columns),
        out_shape=(sds(3, tiles, width, width), sds(3, faces, width)),
        in_specs=[HBM] * 2 + [SMEM] + [VMEM] * 5,
        out_specs=[VMEM] * 2,
        scratch_shapes=[
            pltpu.VMEM((faces, 8, width), f32),
            pltpu.VMEM((3, faces, 8, width), f32),
        ]
        + small,
        cost_estimate=pl.CostEstimate(flops=10**9, bytes_accessed=20 * 10**6, transcendentals=0),
        compiler_params=params(),
    )(counts_hbm, listed, a_table, spread, crowd, cross_sums, face_ghosts, face_rho)
    from_above, from_below, face_force = lax.optimization_barrier(
        (from_above, from_below, face_force)
    )
    force_face = lateral(face_force, -1)
    force_met = pair_force + from_above + from_below
    force_other = swap(force_met[:, upper:])
    force_top = climb(force_met[:, :upper] + force_other, -1)

    force = pl.pallas_call(
        local_force_kernel,
        out_shape=sds(3, tiles, 8, width),
        in_specs=[HBM, HBM, SMEM] + [VMEM] * 5,
        out_specs=VMEM,
        scratch_shapes=[
            pltpu.VMEM((tiles, 8, width), f32),
            pltpu.VMEM((3, tiles, width, width), f32),
            counts_smem,
            pltpu.SMEM(local_nbr.shape, ints),
            pltpu.SemaphoreType.DMA((2,)),
        ],
        cost_estimate=pl.CostEstimate(flops=2 * 10**9, bytes_accessed=20 * 10**6, transcendentals=0),
        compiler_params=params(),
    )(counts_hbm, local_nbr, a_table, payload, spread, crowd, density, ghost_sums)

    return pl.pallas_call(
        finish_kernel,
        out_shape=(sds(*positions.shape), sds(*velocities.shape)),
        in_specs=[SMEM] + [VMEM] * 5,
        out_specs=[VMEM] * 2,
        compiler_params=params(),
    )(counts, positions, velocities, force, force_face, force_top)


def solution(mesh):
    placed = (
        P(None, ("layer", "lat")),
        P(None, ("layer", "lat")),
        P(("layer", "lat")),
        P(("layer", "lat")),
        P(),
        P(("layer", "lat"), None),
        P(("layer", "lat"), None),
        P(("layer", "lat"), None, None),
        P(("layer", "lat"), None),
    )
    return jax.shard_map(
        functools.partial(on_device, mesh.shape["layer"], mesh.shape["lat"]),
        mesh=mesh,
        in_specs=placed,
        out_specs=(P(None, ("layer", "lat")), P(None, ("layer", "lat"))),
        check_vma=False,
    )
```
